32 devices in a mesh: band: 2 (over y), stn: 4 (over z), tm: 4 (over x, core).
Axes of the slice: x: 2, y: 2, z: 4, core: 2. Of those that a mesh axis runs over, the one named last changes fastest.
Arguments:
- samples: bfloat16 [8, 524288], P(('band', 'stn'), 'tm'), parts along dimension 0, may hold values from -6 to 6
- delays: int32 [4, 4], P('stn', 'tm'), may hold values from 0 to 24576, as said below
- fringe: int32 [8, 64], P(('band', 'stn'), 'tm'), parts along dimension 0, may hold values from 0 to 65535
Outputs:
- visibility: float32 [2, 8, 4, 4096], P(None, ('band', 'stn'), None, 'tm'), parts along dimension 1
The draws below stay inside these ranges and needn't reach their ends.
There are 2 independent parts, one for each index of `band`. The reference program is written for one: setup_inputs(seed, part) draws one part's arguments, and reference() takes and returns one part's arrays. A program takes and returns all parts, laid end to end along the dimension named above; an argument that names none is the same for every part. Nothing has to cross between parts.
Inputs may be any that keep to these rules, and one draw needn't show every extreme that they name: delays lie in 0 to 24576; 24576 is reached in every draw.
All inputs are finite; a program needn't handle non-finite values.
Results may differ from the reference program's by a relative error of at most 0.0017.
Values may be sent and summed in bfloat16 or wider, within the bound.
A program may use at most 64 MiB of HBM per device.

```python
import jax
import jax.numpy as jnp
from jax import lax

SPAN = 8192
STATIONS = 4
FR_DEV = 16
FRAMES = 64
NSAMP = 524288
DMAX = 24576
N_TM = 4


def draw_delays(key, part):
    key = jax.random.fold_in(key, 11)
    first_key, second_key = jax.random.split(key)
    values = jax.random.randint(first_key, (STATIONS * N_TM,), 0, DMAX + 1)
    chosen = jax.random.randint(second_key, (), 0, STATIONS * N_TM)
    values = jnp.where(jnp.arange(STATIONS * N_TM) == chosen, DMAX, values)
    return values.reshape(STATIONS, N_TM).astype(jnp.int32)


def plant(entries, key, low, high):
    longest = entries.shape.index(max(entries.shape))
    spots = []
    for shift in (0, 1):
        where = [jax.random.randint(jax.random.fold_in(key, axis), (), 0, length) for axis, length in enumerate(entries.shape)]
        where[longest] = (where[longest] + shift) % entries.shape[longest]
        spots.append(tuple(where))
    return entries.at[spots[0]].set(low).at[spots[1]].set(high)


def levels(rng, extent, cuts, smallest, top_value):
    level = 1.0
    for axis_at, parts in cuts:
        draws = jax.random.uniform(jax.random.fold_in(jax.random.fold_in(rng, 6), axis_at), (parts,), jnp.float32, smallest / len(cuts), top_value / len(cuts))
        level = level * jnp.repeat(jnp.exp(draws), extent[axis_at] // parts).reshape((-1,) + (1,) * (len(extent) - 1 - axis_at))
    return level


def centred(rng, extent, deviation, limit, cuts=(), kind=jnp.bfloat16):
    loudness = levels(rng, extent, cuts, -0.22, 0.18) if cuts else 1.0
    values = jax.random.normal(rng, extent, jnp.float32) * deviation * loudness
    return jnp.minimum(jnp.maximum(values, -limit), limit).astype(kind)


def setup_inputs(seed: int = 0, part: int = 0) -> dict:
    splits = jax.random.split(jax.random.key(seed), 4)
    part_keys = jax.random.split(jax.random.fold_in(splits[3], part), 4)
    samples = centred(part_keys[0], (STATIONS, NSAMP), 1.0, 6.0, ((0, 4), (1, 4)))
    delays = draw_delays(jax.random.fold_in(splits[3], 71), part)
    fringe = plant(jax.random.randint(part_keys[2], (STATIONS, FRAMES), 0, 65536), jax.random.fold_in(part_keys[2], 1), 0, 65535).astype(jnp.int32)
    return {"samples": samples, "delays": delays, "fringe": fringe}


def dft_tables():
    first_index = jnp.arange(64, dtype=jnp.int32)
    second_index = jnp.arange(128, dtype=jnp.int32)
    first_phase = 2.0 * jnp.pi * (first_index[:, None] * first_index[None, :] % 64).astype(jnp.float32) / 64.0
    twist_phase = 2.0 * jnp.pi * (first_index[:, None] * second_index[None, :] % 8192).astype(jnp.float32) / 8192.0
    second_phase = 2.0 * jnp.pi * (second_index[:, None] * first_index[None, :] % 128).astype(jnp.float32) / 128.0
    return (first_phase, twist_phase, second_phase)

def spectrum(aligned, turn_table):
    stations, frames, span = aligned.shape
    first_phase, twist_phase, second_phase = dft_tables()
    high = lax.Precision.HIGHEST
    signal = aligned.astype(jnp.float32).reshape(stations, frames, 64, 128)
    first_real = jnp.einsum('sfab,ak->sfkb', signal, jnp.cos(first_phase), precision=high)
    first_imag = -jnp.einsum('sfab,ak->sfkb', signal, jnp.sin(first_phase), precision=high)
    cos_twist = jnp.cos(twist_phase)
    sin_twist = jnp.sin(twist_phase)
    twist_real = first_real * cos_twist + first_imag * sin_twist
    twist_imag = first_imag * cos_twist - first_real * sin_twist
    cos_second = jnp.cos(second_phase)
    sin_second = jnp.sin(second_phase)
    out_real = jnp.einsum('sfkb,bq->sfqk', twist_real, cos_second, precision=high) + jnp.einsum('sfkb,bq->sfqk', twist_imag, sin_second, precision=high)
    out_imag = jnp.einsum('sfkb,bq->sfqk', twist_imag, cos_second, precision=high) - jnp.einsum('sfkb,bq->sfqk', twist_real, sin_second, precision=high)
    norm_factor = 1.0 / jnp.sqrt(jnp.float32(span))
    out_real = out_real.reshape(stations, frames, span // 2) * norm_factor
    out_imag = out_imag.reshape(stations, frames, span // 2) * norm_factor
    phase_angle = (2.0 * jnp.pi * turn_table.astype(jnp.float32) / 65536.0)[:, :, None]
    cos_fringe = jnp.cos(phase_angle)
    sin_fringe = jnp.sin(phase_angle)
    rotated_real = out_real * cos_fringe + out_imag * sin_fringe
    rotated_imag = out_imag * cos_fringe - out_real * sin_fringe
    return jnp.stack([rotated_real, rotated_imag]).astype(jnp.bfloat16)

def cross(left_spec, right_spec):
    high = lax.Precision.HIGHEST
    left_real = left_spec[0].astype(jnp.float32)
    left_imag = left_spec[1].astype(jnp.float32)
    right_real = right_spec[0].astype(jnp.float32)
    right_imag = right_spec[1].astype(jnp.float32)
    real_part = jnp.einsum('afk,bfk->abk', left_real, right_real, precision=high) + jnp.einsum('afk,bfk->abk', left_imag, right_imag, precision=high)
    imag_part = jnp.einsum('afk,bfk->abk', left_imag, right_real, precision=high) - jnp.einsum('afk,bfk->abk', left_real, right_imag, precision=high)
    return jnp.stack([real_part, imag_part])

def reference(samples, delays, fringe):
    length = FR_DEV * SPAN
    padded = jnp.concatenate([samples, jnp.zeros((STATIONS, DMAX), samples.dtype)], axis=1)
    pieces = []
    for shard in range(N_TM):

        def take(sample_row, shift_by):
            return lax.dynamic_slice_in_dim(sample_row, (shard * length + shift_by).astype(jnp.int32), length)
        pieces.append(jax.vmap(take)(padded, delays[:, shard]))
    aligned = jnp.concatenate(pieces, axis=1).reshape(STATIONS, FRAMES, SPAN)

    def one_station(packed):
        return spectrum(packed[0][None], packed[1][None])[:, 0]
    spectra = lax.map(one_station, (aligned, fringe))
    spectra = jnp.transpose(spectra, (1, 0, 2, 3))
    return cross(spectra, spectra) / jnp.sqrt(jnp.float32(FRAMES))
```

```python
import functools
import math

import jax
import jax.numpy as jnp
import ml_dtypes
import numpy as np
from jax import lax
from jax.experimental import pallas as pl
from jax.experimental.pallas import tpu as pltpu
from jax.sharding import PartitionSpec as P

MESH = pl.DeviceIdType.MESH
SPAN = 8192
DMAX = 24576


def shifted(block, axis, distance):
    devices = range(lax.axis_size(axis))
    route = [(i - distance, i) for i in devices if i - distance in devices]
    return lax.ppermute(block, axis, route)


def passed_along(value, axis, by):
    size = lax.axis_size(axis)
    return lax.ppermute(value, axis, [(i, (i + by) % size) for i in range(size)])


def dft_tables():
    first_index = jnp.arange(64, dtype=jnp.int32)
    second_index = jnp.arange(128, dtype=jnp.int32)
    first_phase = (
        2.0 * jnp.pi * (first_index[:, None] * first_index[None, :] % 64).astype(jnp.float32) / 64.0
    )
    twist_phase = (
        2.0
        * jnp.pi
        * (first_index[:, None] * second_index[None, :] % 8192).astype(jnp.float32)
        / 8192.0
    )
    second_phase = (
        2.0
        * jnp.pi
        * (second_index[:, None] * first_index[None, :] % 128).astype(jnp.float32)
        / 128.0
    )
    return (first_phase, twist_phase, second_phase)


def spectrum(aligned, turn_table):
    stations, frames, span = aligned.shape
    first_phase, twist_phase, second_phase = dft_tables()
    high = lax.Precision.HIGHEST
    signal = aligned.astype(jnp.float32).reshape(stations, frames, 64, 128)
    first_real = jnp.einsum("sfab,ak->sfkb", signal, jnp.cos(first_phase), precision=high)
    first_imag = -jnp.einsum("sfab,ak->sfkb", signal, jnp.sin(first_phase), precision=high)
    cos_twist = jnp.cos(twist_phase)
    sin_twist = jnp.sin(twist_phase)
    twist_real = first_real * cos_twist + first_imag * sin_twist
    twist_imag = first_imag * cos_twist - first_real * sin_twist
    cos_second = jnp.cos(second_phase)
    sin_second = jnp.sin(second_phase)
    out_real = jnp.einsum("sfkb,bq->sfqk", twist_real, cos_second, precision=high) + jnp.einsum(
        "sfkb,bq->sfqk", twist_imag, sin_second, precision=high
    )
    out_imag = jnp.einsum("sfkb,bq->sfqk", twist_imag, cos_second, precision=high) - jnp.einsum(
        "sfkb,bq->sfqk", twist_real, sin_second, precision=high
    )
    norm_factor = 1.0 / jnp.sqrt(jnp.float32(span))
    out_real = out_real.reshape(stations, frames, span // 2) * norm_factor
    out_imag = out_imag.reshape(stations, frames, span // 2) * norm_factor
    phase_angle = (2.0 * jnp.pi * turn_table.astype(jnp.float32) / 65536.0)[:, :, None]
    cos_fringe = jnp.cos(phase_angle)
    sin_fringe = jnp.sin(phase_angle)
    rotated_real = out_real * cos_fringe + out_imag * sin_fringe
    rotated_imag = out_imag * cos_fringe - out_real * sin_fringe
    return jnp.stack([rotated_real, rotated_imag]).astype(jnp.bfloat16)


def cross(left_spec, right_spec):
    f32 = jnp.float32
    real_part = jnp.einsum(
        "afk,bfk->abk", left_spec[0], right_spec[0], preferred_element_type=f32
    ) + jnp.einsum("afk,bfk->abk", left_spec[1], right_spec[1], preferred_element_type=f32)
    imag_part = jnp.einsum(
        "afk,bfk->abk", left_spec[1], right_spec[0], preferred_element_type=f32
    ) - jnp.einsum("afk,bfk->abk", left_spec[0], right_spec[1], preferred_element_type=f32)
    return jnp.stack([real_part, imag_part])


def place(current_totals, block_term, first_station):
    current = lax.dynamic_slice_in_dim(current_totals, first_station, block_term.shape[2], 2)
    return lax.dynamic_update_slice_in_dim(current_totals, current + block_term, first_station, 2)


def on_device(samples, delays, fringe):
    stn_here, length = samples.shape
    frames_here = length // SPAN
    next_head = shifted(samples[:, :DMAX], "tm", -1)
    joined = jnp.concatenate([samples, next_head], axis=1)

    def take(sample_row, shift_by):
        return lax.dynamic_slice_in_dim(sample_row, shift_by, length)

    aligned = jax.vmap(take)(joined, delays[:, 0]).reshape(stn_here, frames_here, SPAN)
    own_spectra = spectrum(aligned, fringe)
    time_count = lax.axis_size("tm")
    channels_now = own_spectra.shape[3]
    cycle_size = lax.axis_size("stn")
    position = lax.axis_index("stn")
    totals = jnp.zeros((2, stn_here, stn_here * cycle_size, channels_now), jnp.float32)
    totals = place(totals, cross(own_spectra, own_spectra), position * stn_here)

    def turn_one(turn_index, state_tuple):
        current_totals, travel = state_tuple
        travel = passed_along(travel, "stn", 1)
        owner_index = (position - turn_index) % cycle_size
        current_totals = place(current_totals, cross(own_spectra, travel), owner_index * stn_here)
        return (current_totals, travel)

    totals, travel_end = lax.fori_loop(1, cycle_size, turn_one, (totals, own_spectra))
    norm_scale = 1.0 / jnp.sqrt(jnp.float32(frames_here * time_count))
    return lax.psum_scatter(totals * norm_scale, "tm", scatter_dimension=3, tiled=True)


LANES = 128
CHUNK = 4


def spectrum_tables(stn_count, tm_count):
    first = np.arange(64)
    second = np.arange(LANES)
    turn = 2.0 * np.pi * (first[:, None] * first[None, :] % 64) / 64.0
    first_table = np.concatenate([np.cos(turn), -np.sin(turn)], axis=0)
    twist = 2.0 * np.pi * (first[:, None] * second[None, :]) / SPAN
    twist_table = np.stack([np.cos(twist), -np.sin(twist)]) / np.sqrt(SPAN)
    rows = []
    for block in range(stn_count * tm_count):
        q = block * 4 + np.array([0, 2, 1, 3])
        turn = 2.0 * np.pi * (q[:, None] * second[None, :] % LANES) / LANES
        rows.append(np.concatenate([np.cos(turn), np.sin(turn)], axis=1))
        rows.append(np.concatenate([-np.sin(turn), np.cos(turn)], axis=1))
    second_table = np.concatenate(rows, axis=0)

    def halves(table):
        high = table.astype(ml_dtypes.bfloat16)
        return high, (table - high.astype(np.float64)).astype(ml_dtypes.bfloat16)

    first_table = np.concatenate(halves(first_table), axis=1)
    second_table = np.concatenate(halves(second_table), axis=0)
    return first_table, twist_table.astype(np.float32), second_table


def fused_kernel(
    S, T, norm_scale,
    samples_ref, delays_ref, fringe_ref, first_ref, twist_ref, second_ref,
    out_ref,
    tail, outgoing, incoming, pieces, landed,
    halo_sems, send_sems, recv_sems, last_send_sems, last_recv_sems,
):
    f32, bf16 = jnp.float32, jnp.bfloat16
    band = lax.axis_index("band")
    s_me = lax.axis_index("stn")
    t_me = lax.axis_index("tm")
    partners = [(ds, dt) for ds in (2, 3, 1, 0) for dt in range(T) if (ds, dt) != (0, 0)]
    rows_chunk = CHUNK * 64
    chunks = samples_ref.shape[0] // rows_chunk
    halo_rows = DMAX // LANES
    tail_start = (chunks - 1) * rows_chunk

    def partner(ds, dt):
        return lax.rem(s_me + ds, S), lax.rem(t_me + dt, T)

    barrier = pltpu.get_barrier_semaphore()
    for ds, dt in partners:
        s_to, t_to = partner(ds, dt)
        pl.semaphore_signal(barrier, inc=1, device_id=(band, s_to, t_to), device_id_type=MESH)

    tail[pl.ds(0, rows_chunk), :] = samples_ref[pl.ds(tail_start, rows_chunk), :]
    tail[pl.ds(rows_chunk + halo_rows, 8), :] = jnp.zeros((8, LANES), f32)

    @pl.when(t_me == T - 1)
    def _():
        tail[pl.ds(rows_chunk, halo_rows), :] = jnp.zeros((halo_rows, LANES), f32)

    delay = delays_ref[0, 0]
    delay_rows = delay // LANES
    delay_lanes = delay - delay_rows * LANES
    lane_from = lax.broadcasted_iota(jnp.int32, (2 * LANES, LANES), 0)
    lane_to = lax.broadcasted_iota(jnp.int32, (2 * LANES, LANES), 1)
    shift = jnp.where(lane_from == lane_to + delay_lanes, 1.0, 0.0).astype(bf16)

    phase = fringe_ref[...].astype(f32) * (2.0 * math.pi / 65536.0)
    cos_fringe = jnp.cos(phase)
    sin_fringe = jnp.sin(phase)

    def chunk_spectra(c):
        source, start = (tail, 0) if c == chunks - 1 else (samples_ref, c * rows_chunk)
        here = source[pl.ds(delay_rows + start, rows_chunk), :].astype(bf16)
        after = source[pl.ds(delay_rows + (start + 1), rows_chunk), :].astype(bf16)
        aligned = jnp.dot(
            jnp.concatenate([here, after], axis=1), shift, preferred_element_type=f32
        ).astype(bf16)
        frames = [aligned[64 * f : 64 * (f + 1)] for f in range(CHUNK)]
        side = jnp.concatenate(frames, axis=1)
        first = jnp.dot(
            first_ref[...], jnp.concatenate([side, side], axis=0), preferred_element_type=f32
        )
        twisted = []
        for f in range(CHUNK):
            at = c * CHUNK + f
            cos_f = cos_fringe[:, at : at + 1]
            sin_f = sin_fringe[:, at : at + 1]
            twist_real = twist_ref[0] * cos_f + twist_ref[1] * sin_f
            twist_imag = twist_ref[1] * cos_f - twist_ref[0] * sin_f
            real = first[:64, LANES * f : LANES * (f + 1)]
            imag = first[64:, LANES * f : LANES * (f + 1)]
            twisted.append(
                jnp.concatenate(
                    [
                        real * twist_real - imag * twist_imag,
                        real * twist_imag + imag * twist_real,
                    ],
                    axis=1,
                )
            )
        twisted = jnp.concatenate(twisted, axis=0)
        high = twisted.astype(bf16)
        low = (twisted - high.astype(f32)).astype(bf16)
        across = (((1,), (1,)), ((), ()))
        both = lax.dot_general(second_ref[...], high, across, preferred_element_type=f32)
        small = lax.dot_general(second_ref[:LANES], low, across, preferred_element_type=f32)
        spectra = both[:LANES] + (both[LANES:] + small)
        blocks = jnp.concatenate(
            [
                spectra[:, :LANES].reshape(S * T, 8, LANES),
                spectra[:, LANES:].reshape(S * T, 8, LANES),
            ],
            axis=1,
        )
        outgoing[c] = blocks.astype(bf16)

    def spectra_copy(c, ds, dt):
        s_to, t_to = partner(ds, dt)
        return pltpu.make_async_remote_copy(
            src_ref=outgoing.at[c, t_to * S + s_to],
            dst_ref=incoming.at[c, s_me, dt],
            send_sem=send_sems.at[c, ds, dt],
            recv_sem=recv_sems.at[c, ds, dt],
            device_id=(band, s_to, t_to),
            device_id_type=MESH,
        )

    def halo_copy():
        return pltpu.make_async_remote_copy(
            src_ref=samples_ref.at[pl.ds(0, halo_rows)],
            dst_ref=tail.at[pl.ds(rows_chunk, halo_rows)],
            send_sem=halo_sems.at[0],
            recv_sem=halo_sems.at[1],
            device_id=(band, s_me, lax.rem(t_me + T - 1, T)),
            device_id_type=MESH,
        )

    for c in range(chunks):
        if c == chunks - 1:

            @pl.when(t_me < T - 1)
            def _():
                halo_copy().wait_recv()

        chunk_spectra(c)
        if c == 0:
            pl.semaphore_wait(barrier, len(partners))

            @pl.when(t_me > 0)
            def _():
                halo_copy().start()

        for ds, dt in partners:
            spectra_copy(c, ds, dt).start()
        incoming[c, s_me, 0] = outgoing[c, t_me * S + s_me]

    pairs = [(i, j) for i in range(S) for j in range(i, S)]
    even = {pair: jnp.zeros((8, LANES), f32) for pair in pairs}
    odd = {pair: jnp.zeros((8, LANES), f32) for pair in pairs if pair[0] != pair[1]}
    for c in range(chunks):
        for ds, dt in partners:
            spectra_copy(c, ds, dt).wait_recv()
        for dt in range(T):
            tiles = [incoming[c, s, dt].astype(f32) for s in range(S)]
            for half in range(2):
                part = [tile[8 * half : 8 * half + 8] for tile in tiles]
                turned = [None] + [pltpu.roll(p, 4, 0) for p in part[1:]]
                for i, j in pairs:
                    even[i, j] += part[i] * part[j]
                    if i != j:
                        odd[i, j] += part[i] * turned[j]

    left = lax.broadcasted_iota(jnp.int32, (8, LANES), 1) < 64

    def settle(total, sign):
        total = total + pltpu.roll(total, 64, 1)
        total = (pltpu.roll(total, 4, 0) + sign * total) * norm_scale
        return jnp.where(left, total, pltpu.roll(total, 6, 0))

    def put(i, row, value):
        pieces[i, pl.ds(row, 1), pl.ds(0, LANES)] = value[0:1]
        pieces[i, pl.ds(row, 1), pl.ds(LANES, LANES)] = value[1:2]

    for i, j in pairs:
        real = settle(even[i, j], 1.0)
        put(i, j, real)
        if i == j:
            put(i, S + i, jnp.zeros_like(real))
        else:
            put(j, i, real)
            imag = settle(odd[i, j], -1.0)
            put(i, S + j, imag)
            put(j, S + i, -imag)

    def last_copy(ds):
        s_to = lax.rem(s_me + ds, S)
        return pltpu.make_async_remote_copy(
            src_ref=pieces.at[s_to],
            dst_ref=landed.at[s_me],
            send_sem=last_send_sems.at[ds],
            recv_sem=last_recv_sems.at[ds],
            device_id=(band, s_to, t_me),
            device_id_type=MESH,
        )

    for ds in (2, 3, 1):
        last_copy(ds).start()
    landed[s_me] = pieces[s_me]
    for ds in (2, 3, 1):
        last_copy(ds).wait_recv()
    for s in range(S):
        out_ref[:, pl.ds(s * 2 * LANES, 2 * LANES)] = landed[s]

    for ds in (2, 3, 1):
        last_copy(ds).wait_send()
    for c in range(chunks):
        for ds, dt in partners:
            spectra_copy(c, ds, dt).wait_send()

    @pl.when(t_me > 0)
    def _():
        halo_copy().wait_send()


def fused_on_device(stn_count, tm_count, samples, delays, fringe):
    length = samples.shape[1]
    rows = length // LANES
    chunks = rows // (CHUNK * 64)
    blocks = stn_count * tm_count
    signal = samples.astype(jnp.float32).reshape(rows, LANES)
    first_table, twist_table, second_table = spectrum_tables(stn_count, tm_count)
    norm_scale = 1.0 / math.sqrt(length // SPAN * tm_count)
    vmem = pl.BlockSpec(memory_space=pltpu.VMEM)
    smem = pl.BlockSpec(memory_space=pltpu.SMEM)
    out = pl.pallas_call(
        functools.partial(fused_kernel, stn_count, tm_count, norm_scale),
        out_shape=jax.ShapeDtypeStruct((2 * stn_count, 1024), jnp.float32),
        in_specs=[vmem, smem, vmem, vmem, vmem, vmem],
        out_specs=vmem,
        scratch_shapes=[
            pltpu.VMEM((CHUNK * 64 + DMAX // LANES + 8, LANES), jnp.float32),
            pltpu.VMEM((chunks, blocks, 16, LANES), jnp.bfloat16),
            pltpu.VMEM((chunks, stn_count, tm_count, 16, LANES), jnp.bfloat16),
            pltpu.VMEM((stn_count, 2 * stn_count, 2 * LANES), jnp.float32),
            pltpu.VMEM((stn_count, 2 * stn_count, 2 * LANES), jnp.float32),
            pltpu.SemaphoreType.DMA((2,)),
            pltpu.SemaphoreType.DMA((chunks, stn_count, tm_count)),
            pltpu.SemaphoreType.DMA((chunks, stn_count, tm_count)),
            pltpu.SemaphoreType.DMA((stn_count,)),
            pltpu.SemaphoreType.DMA((stn_count,)),
        ],
        compiler_params=pltpu.CompilerParams(
            collective_id=0, has_side_effects=True, vmem_limit_bytes=32 << 20
        ),
        name="correlate",
    )(signal, delays, fringe, jnp.asarray(first_table), jnp.asarray(twist_table), jnp.asarray(second_table))
    return out.reshape(2, 1, stn_count, 1024)


def solution(mesh):
    stn_count, tm_count = mesh.shape["stn"], mesh.shape["tm"]
    body = on_device
    if (stn_count, tm_count) == (4, 4):
        body = functools.partial(fused_on_device, stn_count, tm_count)
    return jax.shard_map(
        body,
        mesh=mesh,
        in_specs=(P(("band", "stn"), "tm"), P("stn", "tm"), P(("band", "stn"), "tm")),
        out_specs=P(None, ("band", "stn"), None, "tm"),
        check_vma=False,
    )
```

```python
import functools
import math

import jax
import jax.numpy as jnp
import ml_dtypes
import numpy as np
from jax import lax
from jax.experimental import pallas as pl
from jax.experimental.pallas import tpu as pltpu
from jax.sharding import PartitionSpec as P

MESH = pl.DeviceIdType.MESH
SPAN = 8192
DMAX = 24576


def shifted(block, axis, distance):
    devices = range(lax.axis_size(axis))
    route = [(i - distance, i) for i in devices if i - distance in devices]
    return lax.ppermute(block, axis, route)


def passed_along(value, axis, by):
    size = lax.axis_size(axis)
    return lax.ppermute(value, axis, [(i, (i + by) % size) for i in range(size)])


def dft_tables():
    first_index = jnp.arange(64, dtype=jnp.int32)
    second_index = jnp.arange(128, dtype=jnp.int32)
    first_phase = (
        2.0 * jnp.pi * (first_index[:, None] * first_index[None, :] % 64).astype(jnp.float32) / 64.0
    )
    twist_phase = (
        2.0
        * jnp.pi
        * (first_index[:, None] * second_index[None, :] % 8192).astype(jnp.float32)
        / 8192.0
    )
    second_phase = (
        2.0
        * jnp.pi
        * (second_index[:, None] * first_index[None, :] % 128).astype(jnp.float32)
        / 128.0
    )
    return (first_phase, twist_phase, second_phase)


def spectrum(aligned, turn_table):
    stations, frames, span = aligned.shape
    first_phase, twist_phase, second_phase = dft_tables()
    high = lax.Precision.HIGHEST
    signal = aligned.astype(jnp.float32).reshape(stations, frames, 64, 128)
    first_real = jnp.einsum("sfab,ak->sfkb", signal, jnp.cos(first_phase), precision=high)
    first_imag = -jnp.einsum("sfab,ak->sfkb", signal, jnp.sin(first_phase), precision=high)
    cos_twist = jnp.cos(twist_phase)
    sin_twist = jnp.sin(twist_phase)
    twist_real = first_real * cos_twist + first_imag * sin_twist
    twist_imag = first_imag * cos_twist - first_real * sin_twist
    cos_second = jnp.cos(second_phase)
    sin_second = jnp.sin(second_phase)
    out_real = jnp.einsum("sfkb,bq->sfqk", twist_real, cos_second, precision=high) + jnp.einsum(
        "sfkb,bq->sfqk", twist_imag, sin_second, precision=high
    )
    out_imag = jnp.einsum("sfkb,bq->sfqk", twist_imag, cos_second, precision=high) - jnp.einsum(
        "sfkb,bq->sfqk", twist_real, sin_second, precision=high
    )
    norm_factor = 1.0 / jnp.sqrt(jnp.float32(span))
    out_real = out_real.reshape(stations, frames, span // 2) * norm_factor
    out_imag = out_imag.reshape(stations, frames, span // 2) * norm_factor
    phase_angle = (2.0 * jnp.pi * turn_table.astype(jnp.float32) / 65536.0)[:, :, None]
    cos_fringe = jnp.cos(phase_angle)
    sin_fringe = jnp.sin(phase_angle)
    rotated_real = out_real * cos_fringe + out_imag * sin_fringe
    rotated_imag = out_imag * cos_fringe - out_real * sin_fringe
    return jnp.stack([rotated_real, rotated_imag]).astype(jnp.bfloat16)


def cross(left_spec, right_spec):
    f32 = jnp.float32
    real_part = jnp.einsum(
        "afk,bfk->abk", left_spec[0], right_spec[0], preferred_element_type=f32
    ) + jnp.einsum("afk,bfk->abk", left_spec[1], right_spec[1], preferred_element_type=f32)
    imag_part = jnp.einsum(
        "afk,bfk->abk", left_spec[1], right_spec[0], preferred_element_type=f32
    ) - jnp.einsum("afk,bfk->abk", left_spec[0], right_spec[1], preferred_element_type=f32)
    return jnp.stack([real_part, imag_part])


def place(current_totals, block_term, first_station):
    current = lax.dynamic_slice_in_dim(current_totals, first_station, block_term.shape[2], 2)
    return lax.dynamic_update_slice_in_dim(current_totals, current + block_term, first_station, 2)


def on_device(samples, delays, fringe):
    stn_here, length = samples.shape
    frames_here = length // SPAN
    next_head = shifted(samples[:, :DMAX], "tm", -1)
    joined = jnp.concatenate([samples, next_head], axis=1)

    def take(sample_row, shift_by):
        return lax.dynamic_slice_in_dim(sample_row, shift_by, length)

    aligned = jax.vmap(take)(joined, delays[:, 0]).reshape(stn_here, frames_here, SPAN)
    own_spectra = spectrum(aligned, fringe)
    time_count = lax.axis_size("tm")
    channels_now = own_spectra.shape[3]
    cycle_size = lax.axis_size("stn")
    position = lax.axis_index("stn")
    totals = jnp.zeros((2, stn_here, stn_here * cycle_size, channels_now), jnp.float32)
    totals = place(totals, cross(own_spectra, own_spectra), position * stn_here)

    def turn_one(turn_index, state_tuple):
        current_totals, travel = state_tuple
        travel = passed_along(travel, "stn", 1)
        owner_index = (position - turn_index) % cycle_size
        current_totals = place(current_totals, cross(own_spectra, travel), owner_index * stn_here)
        return (current_totals, travel)

    totals, travel_end = lax.fori_loop(1, cycle_size, turn_one, (totals, own_spectra))
    norm_scale = 1.0 / jnp.sqrt(jnp.float32(frames_here * time_count))
    return lax.psum_scatter(totals * norm_scale, "tm", scatter_dimension=3, tiled=True)


LANES = 128
CHUNK = 4
GROUPS = ((0, 0), (1, 1), (2, 2), (3, 3))


def spectrum_tables(stn_count, tm_count):
    first = np.arange(64)
    second = np.arange(LANES)
    turn = 2.0 * np.pi * (first[:, None] * first[None, :] % 64) / 64.0
    first_table = np.concatenate([np.cos(turn), -np.sin(turn)], axis=0)
    twist = 2.0 * np.pi * (first[:, None] * second[None, :]) / SPAN
    twist_table = np.stack([np.cos(twist), -np.sin(twist)]) / np.sqrt(SPAN)
    rows = []
    for block in range(stn_count * tm_count):
        q = block * 4 + np.array([0, 2, 1, 3])
        turn = 2.0 * np.pi * (q[:, None] * second[None, :] % LANES) / LANES
        rows.append(np.concatenate([np.cos(turn), np.sin(turn)], axis=1))
        rows.append(np.concatenate([-np.sin(turn), np.cos(turn)], axis=1))
    second_table = np.concatenate(rows, axis=0)

    def halves(table):
        high = table.astype(ml_dtypes.bfloat16)
        return high, (table - high.astype(np.float64)).astype(ml_dtypes.bfloat16)

    first_table = np.concatenate(halves(first_table), axis=1)
    second_table = np.concatenate(halves(second_table), axis=0)
    return first_table, twist_table.astype(np.float32), second_table


def fused_kernel(
    S, T, norm_scale,
    samples_hbm, delays_hbm, fringe_hbm, first_hbm, twist_hbm, second_hbm,
    out_ref,
    flat, delays_ref, fringe_ref, first_ref, twist_ref, second_ref,
    signal, tail, outgoing, incoming, pieces, landed,
    load_sems, halo_sems, send_sem, recv_sems, last_sems,
):
    f32, bf16 = jnp.float32, jnp.bfloat16
    band = lax.axis_index("band")
    s_me = lax.axis_index("stn")
    t_me = lax.axis_index("tm")
    partners = [(ds, dt) for ds in (2, 3, 1, 0) for dt in range(T) if (ds, dt) != (0, 0)]
    rows_chunk = CHUNK * 64
    chunks = signal.shape[0] // rows_chunk
    halo_rows = DMAX // LANES
    tail_start = (chunks - 1) * rows_chunk

    def partner(ds, dt):
        return lax.rem(s_me + ds, S), lax.rem(t_me + dt, T)

    half = flat.shape[1] // 2
    loads = [
        pltpu.make_async_copy(source, target, load_sems.at[index])
        for index, (source, target) in enumerate(
            [
                (samples_hbm.at[:, pl.ds(0, half)], flat.at[:, pl.ds(0, half)]),
                (delays_hbm, delays_ref),
                (first_hbm, first_ref),
                (fringe_hbm, fringe_ref),
                (twist_hbm, twist_ref),
                (second_hbm, second_ref),
                (samples_hbm.at[:, pl.ds(half, half)], flat.at[:, pl.ds(half, half)]),
            ]
        )
    ]
    for load in loads:
        load.start()

    barrier = pltpu.get_barrier_semaphore()
    for ds, dt in partners:
        s_to, t_to = partner(ds, dt)
        pl.semaphore_signal(barrier, inc=1, device_id=(band, s_to, t_to), device_id_type=MESH)

    tail[pl.ds(rows_chunk + halo_rows, 8), :] = jnp.zeros((8, LANES), f32)

    @pl.when(t_me == T - 1)
    def _():
        tail[pl.ds(rows_chunk, halo_rows), :] = jnp.zeros((halo_rows, LANES), f32)

    def lay_out(first_row, row_count):
        for row in range(first_row, first_row + row_count, 64):
            part = flat[:, pl.ds(row * LANES, 64 * LANES)].astype(f32).reshape(64, LANES)
            signal[pl.ds(row, 64), :] = part
            if row >= tail_start:
                tail[pl.ds(row - tail_start, 64), :] = part

    loads[0].wait()
    lay_out(0, 2 * rows_chunk)
    loads[1].wait()
    loads[2].wait()
    loads[3].wait()
    delay = delays_ref[0, 0]
    delay_rows = delay // LANES
    delay_lanes = delay - delay_rows * LANES
    lane_from = lax.broadcasted_iota(jnp.int32, (2 * LANES, LANES), 0)
    lane_to = lax.broadcasted_iota(jnp.int32, (2 * LANES, LANES), 1)
    shift = jnp.where(lane_from == lane_to + delay_lanes, 1.0, 0.0).astype(bf16)

    phase = fringe_ref[...].astype(f32) * (2.0 * math.pi / 65536.0)
    cos_fringe = jnp.cos(phase)
    sin_fringe = jnp.sin(phase)

    def chunk_spectra(c):
        source, start = (tail, 0) if c == chunks - 1 else (signal, c * rows_chunk)
        here = source[pl.ds(delay_rows + start, rows_chunk), :].astype(bf16)
        after = source[pl.ds(delay_rows + (start + 1), rows_chunk), :].astype(bf16)
        aligned = jnp.dot(
            jnp.concatenate([here, after], axis=1), shift, preferred_element_type=f32
        ).astype(bf16)
        frames = [aligned[64 * f : 64 * (f + 1)] for f in range(CHUNK)]
        side = jnp.concatenate(frames, axis=1)
        first = jnp.dot(
            first_ref[...], jnp.concatenate([side, side], axis=0), preferred_element_type=f32
        )
        twisted = []
        for f in range(CHUNK):
            at = c * CHUNK + f
            cos_f = cos_fringe[:, at : at + 1]
            sin_f = sin_fringe[:, at : at + 1]
            twist_real = twist_ref[0] * cos_f + twist_ref[1] * sin_f
            twist_imag = twist_ref[1] * cos_f - twist_ref[0] * sin_f
            real = first[:64, LANES * f : LANES * (f + 1)]
            imag = first[64:, LANES * f : LANES * (f + 1)]
            twisted.append(
                jnp.concatenate(
                    [
                        real * twist_real - imag * twist_imag,
                        real * twist_imag + imag * twist_real,
                    ],
                    axis=1,
                )
            )
        twisted = jnp.concatenate(twisted, axis=0)
        high = twisted.astype(bf16)
        low = (twisted - high.astype(f32)).astype(bf16)
        across = (((1,), (1,)), ((), ()))
        both = lax.dot_general(second_ref[...], high, across, preferred_element_type=f32)
        small = lax.dot_general(second_ref[:LANES], low, across, preferred_element_type=f32)
        spectra = both[:LANES] + (both[LANES:] + small)
        outgoing[:, c] = jnp.concatenate(
            [
                spectra[:, :LANES].reshape(S * T, 8, LANES),
                spectra[:, LANES:].reshape(S * T, 8, LANES),
            ],
            axis=1,
        ).astype(bf16)

    def spectra_copy(group, ds, dt):
        s_to, t_to = partner(ds, dt)
        first_chunk, last_chunk = GROUPS[group]
        part = pl.ds(first_chunk, last_chunk + 1 - first_chunk)
        return pltpu.make_async_remote_copy(
            src_ref=outgoing.at[t_to * S + s_to, part],
            dst_ref=incoming.at[s_me * T + dt, part],
            send_sem=send_sem,
            recv_sem=recv_sems.at[group],
            device_id=(band, s_to, t_to),
            device_id_type=MESH,
        )

    def all_arrived(group):
        first_chunk, last_chunk = GROUPS[group]
        part = incoming.at[pl.ds(0, S * T - 1), pl.ds(first_chunk, last_chunk + 1 - first_chunk)]
        pltpu.make_async_copy(part, part, recv_sems.at[group]).wait()

    def halo_copy():
        return pltpu.make_async_remote_copy(
            src_ref=signal.at[pl.ds(0, halo_rows)],
            dst_ref=tail.at[pl.ds(rows_chunk, halo_rows)],
            send_sem=halo_sems.at[0],
            recv_sem=halo_sems.at[1],
            device_id=(band, s_me, lax.rem(t_me + T - 1, T)),
            device_id_type=MESH,
        )

    for c in range(chunks):
        if c == 0:
            loads[4].wait()
            loads[5].wait()
        elif c == 1:
            loads[6].wait()
            lay_out(2 * rows_chunk, rows_chunk)
        elif c == 2:
            lay_out(3 * rows_chunk, rows_chunk)
        else:

            @pl.when(t_me < T - 1)
            def _():
                halo_copy().wait_recv()

        chunk_spectra(c)
        if c == 0:
            pl.semaphore_wait(barrier, len(partners))

            @pl.when(t_me > 0)
            def _():
                halo_copy().start()

        for group, (_, last_chunk) in enumerate(GROUPS):
            if last_chunk == c:
                for ds, dt in partners:
                    spectra_copy(group, ds, dt).start()
        incoming[s_me * T, c] = outgoing[t_me * S + s_me, c]

    pairs = [(i, j) for i in range(S) for j in range(i, S)]
    even = {pair: jnp.zeros((8, LANES), f32) for pair in pairs}
    odd = {pair: jnp.zeros((8, LANES), f32) for pair in pairs if pair[0] != pair[1]}
    for group, (first_chunk, last_chunk) in enumerate(GROUPS):
        all_arrived(group)
        for dt, c in [(dt, c) for dt in range(T) for c in range(first_chunk, last_chunk + 1)]:
            tiles = [incoming[s * T + dt, c].astype(f32) for s in range(S)]
            for top in (0, 8):
                part = [tile[top : top + 8] for tile in tiles]
                turned = [None] + [pltpu.roll(p, 4, 0) for p in part[1:]]
                for i, j in pairs:
                    even[i, j] += part[i] * part[j]
                    if i != j:
                        odd[i, j] += part[i] * turned[j]

    left = lax.broadcasted_iota(jnp.int32, (8, LANES), 1) < 64

    def settle(total, sign):
        total = total + pltpu.roll(total, 64, 1)
        total = (pltpu.roll(total, 4, 0) + sign * total) * norm_scale
        return jnp.where(left, total, pltpu.roll(total, 6, 0))

    def put(i, row, value):
        pieces[i, pl.ds(row, 1), pl.ds(0, LANES)] = value[0:1]
        pieces[i, pl.ds(row, 1), pl.ds(LANES, LANES)] = value[1:2]

    for i, j in pairs:
        real = settle(even[i, j], 1.0)
        put(i, j, real)
        if i == j:
            put(i, S + i, jnp.zeros_like(real))
        else:
            put(j, i, real)
            imag = settle(odd[i, j], -1.0)
            put(i, S + j, imag)
            put(j, S + i, -imag)

    def last_copy(ds):
        s_to = lax.rem(s_me + ds, S)
        return pltpu.make_async_remote_copy(
            src_ref=pieces.at[s_to],
            dst_ref=landed.at[s_me],
            send_sem=last_sems.at[0],
            recv_sem=last_sems.at[1],
            device_id=(band, s_to, t_me),
            device_id_type=MESH,
        )

    for ds in (2, 3, 1):
        last_copy(ds).start()
    landed[s_me] = pieces[s_me]
    others = landed.at[pl.ds(0, S - 1)]
    pltpu.make_async_copy(others, others, last_sems.at[1]).wait()
    for s in range(S):
        out_ref[:, pl.ds(s * 2 * LANES, 2 * LANES)] = landed[s]

    pltpu.make_async_copy(others, others, last_sems.at[0]).wait()
    sent = outgoing.at[pl.ds(0, S * T - 1)]
    pltpu.make_async_copy(sent, sent, send_sem).wait()

    @pl.when(t_me > 0)
    def _():
        halo_copy().wait_send()


def fused_on_device(stn_count, tm_count, samples, delays, fringe):
    length = samples.shape[1]
    rows = length // LANES
    chunks = rows // (CHUNK * 64)
    blocks = stn_count * tm_count
    norm_scale = 1.0 / math.sqrt(length // SPAN * tm_count)
    tables = spectrum_tables(stn_count, tm_count)
    operands = [samples, delays, fringe] + [jnp.asarray(table) for table in tables]
    out = pl.pallas_call(
        functools.partial(fused_kernel, stn_count, tm_count, norm_scale),
        out_shape=jax.ShapeDtypeStruct((2 * stn_count, 1024), jnp.float32),
        in_specs=[pl.BlockSpec(memory_space=pltpu.HBM)] * len(operands),
        out_specs=pl.BlockSpec(memory_space=pltpu.VMEM),
        scratch_shapes=[
            pltpu.VMEM(samples.shape, samples.dtype),
            pltpu.SMEM(delays.shape, delays.dtype),
        ]
        + [pltpu.VMEM(operand.shape, operand.dtype) for operand in operands[2:]]
        + [
            pltpu.VMEM((rows, LANES), jnp.float32),
            pltpu.VMEM((CHUNK * 64 + DMAX // LANES + 8, LANES), jnp.float32),
            pltpu.VMEM((blocks, chunks, 16, LANES), jnp.bfloat16),
            pltpu.VMEM((blocks, chunks, 16, LANES), jnp.bfloat16),
            pltpu.VMEM((stn_count, 2 * stn_count, 2 * LANES), jnp.float32),
            pltpu.VMEM((stn_count, 2 * stn_count, 2 * LANES), jnp.float32),
            pltpu.SemaphoreType.DMA((7,)),
            pltpu.SemaphoreType.DMA((2,)),
            pltpu.SemaphoreType.DMA,
            pltpu.SemaphoreType.DMA((len(GROUPS),)),
            pltpu.SemaphoreType.DMA((2,)),
        ],
        compiler_params=pltpu.CompilerParams(
            collective_id=0, has_side_effects=True, vmem_limit_bytes=60 << 20
        ),
        name="correlate",
    )(*operands)
    return out.reshape(2, 1, stn_count, 1024)


def solution(mesh):
    stn_count, tm_count = mesh.shape["stn"], mesh.shape["tm"]
    body = on_device
    if (stn_count, tm_count) == (4, 4):
        body = functools.partial(fused_on_device, stn_count, tm_count)
    return jax.shard_map(
        body,
        mesh=mesh,
        in_specs=(P(("band", "stn"), "tm"), P("stn", "tm"), P(("band", "stn"), "tm")),
        out_specs=P(None, ("band", "stn"), None, "tm"),
        check_vma=False,
    )
```

```python
import functools
import math

import jax
import jax.numpy as jnp
import ml_dtypes
import numpy as np
from jax import lax
from jax.experimental import pallas as pl
from jax.experimental.pallas import tpu as pltpu
from jax.sharding import PartitionSpec as P

MESH = pl.DeviceIdType.MESH
SPAN = 8192
DMAX = 24576


def shifted(block, axis, distance):
    devices = range(lax.axis_size(axis))
    route = [(i - distance, i) for i in devices if i - distance in devices]
    return lax.ppermute(block, axis, route)


def passed_along(value, axis, by):
    size = lax.axis_size(axis)
    return lax.ppermute(value, axis, [(i, (i + by) % size) for i in range(size)])


def dft_tables():
    first_index = jnp.arange(64, dtype=jnp.int32)
    second_index = jnp.arange(128, dtype=jnp.int32)
    first_phase = (
        2.0 * jnp.pi * (first_index[:, None] * first_index[None, :] % 64).astype(jnp.float32) / 64.0
    )
    twist_phase = (
        2.0
        * jnp.pi
        * (first_index[:, None] * second_index[None, :] % 8192).astype(jnp.float32)
        / 8192.0
    )
    second_phase = (
        2.0
        * jnp.pi
        * (second_index[:, None] * first_index[None, :] % 128).astype(jnp.float32)
        / 128.0
    )
    return (first_phase, twist_phase, second_phase)


def spectrum(aligned, turn_table):
    stations, frames, span = aligned.shape
    first_phase, twist_phase, second_phase = dft_tables()
    high = lax.Precision.HIGHEST
    signal = aligned.astype(jnp.float32).reshape(stations, frames, 64, 128)
    first_real = jnp.einsum("sfab,ak->sfkb", signal, jnp.cos(first_phase), precision=high)
    first_imag = -jnp.einsum("sfab,ak->sfkb", signal, jnp.sin(first_phase), precision=high)
    cos_twist = jnp.cos(twist_phase)
    sin_twist = jnp.sin(twist_phase)
    twist_real = first_real * cos_twist + first_imag * sin_twist
    twist_imag = first_imag * cos_twist - first_real * sin_twist
    cos_second = jnp.cos(second_phase)
    sin_second = jnp.sin(second_phase)
    out_real = jnp.einsum("sfkb,bq->sfqk", twist_real, cos_second, precision=high) + jnp.einsum(
        "sfkb,bq->sfqk", twist_imag, sin_second, precision=high
    )
    out_imag = jnp.einsum("sfkb,bq->sfqk", twist_imag, cos_second, precision=high) - jnp.einsum(
        "sfkb,bq->sfqk", twist_real, sin_second, precision=high
    )
    norm_factor = 1.0 / jnp.sqrt(jnp.float32(span))
    out_real = out_real.reshape(stations, frames, span // 2) * norm_factor
    out_imag = out_imag.reshape(stations, frames, span // 2) * norm_factor
    phase_angle = (2.0 * jnp.pi * turn_table.astype(jnp.float32) / 65536.0)[:, :, None]
    cos_fringe = jnp.cos(phase_angle)
    sin_fringe = jnp.sin(phase_angle)
    rotated_real = out_real * cos_fringe + out_imag * sin_fringe
    rotated_imag = out_imag * cos_fringe - out_real * sin_fringe
    return jnp.stack([rotated_real, rotated_imag]).astype(jnp.bfloat16)


def cross(left_spec, right_spec):
    f32 = jnp.float32
    real_part = jnp.einsum(
        "afk,bfk->abk", left_spec[0], right_spec[0], preferred_element_type=f32
    ) + jnp.einsum("afk,bfk->abk", left_spec[1], right_spec[1], preferred_element_type=f32)
    imag_part = jnp.einsum(
        "afk,bfk->abk", left_spec[1], right_spec[0], preferred_element_type=f32
    ) - jnp.einsum("afk,bfk->abk", left_spec[0], right_spec[1], preferred_element_type=f32)
    return jnp.stack([real_part, imag_part])


def place(current_totals, block_term, first_station):
    current = lax.dynamic_slice_in_dim(current_totals, first_station, block_term.shape[2], 2)
    return lax.dynamic_update_slice_in_dim(current_totals, current + block_term, first_station, 2)


def on_device(samples, delays, fringe):
    stn_here, length = samples.shape
    frames_here = length // SPAN
    next_head = shifted(samples[:, :DMAX], "tm", -1)
    joined = jnp.concatenate([samples, next_head], axis=1)

    def take(sample_row, shift_by):
        return lax.dynamic_slice_in_dim(sample_row, shift_by, length)

    aligned = jax.vmap(take)(joined, delays[:, 0]).reshape(stn_here, frames_here, SPAN)
    own_spectra = spectrum(aligned, fringe)
    time_count = lax.axis_size("tm")
    channels_now = own_spectra.shape[3]
    cycle_size = lax.axis_size("stn")
    position = lax.axis_index("stn")
    totals = jnp.zeros((2, stn_here, stn_here * cycle_size, channels_now), jnp.float32)
    totals = place(totals, cross(own_spectra, own_spectra), position * stn_here)

    def turn_one(turn_index, state_tuple):
        current_totals, travel = state_tuple
        travel = passed_along(travel, "stn", 1)
        owner_index = (position - turn_index) % cycle_size
        current_totals = place(current_totals, cross(own_spectra, travel), owner_index * stn_here)
        return (current_totals, travel)

    totals, travel_end = lax.fori_loop(1, cycle_size, turn_one, (totals, own_spectra))
    norm_scale = 1.0 / jnp.sqrt(jnp.float32(frames_here * time_count))
    return lax.psum_scatter(totals * norm_scale, "tm", scatter_dimension=3, tiled=True)


LANES = 128
CHUNK = 4


def spectrum_tables(stn_count, tm_count):
    first = np.arange(64)
    second = np.arange(LANES)
    turn = 2.0 * np.pi * (first[:, None] * first[None, :] % 64) / 64.0
    first_table = np.concatenate([np.cos(turn), -np.sin(turn)], axis=0)
    twist = 2.0 * np.pi * (first[:, None] * second[None, :]) / SPAN
    twist_table = np.stack([np.cos(twist), -np.sin(twist)]) / np.sqrt(SPAN)
    rows = []
    for block in range(stn_count * tm_count):
        q = block * 4 + np.array([0, 2, 1, 3])
        turn = 2.0 * np.pi * (q[:, None] * second[None, :] % LANES) / LANES
        rows.append(np.concatenate([np.cos(turn), np.sin(turn)], axis=1))
        rows.append(np.concatenate([-np.sin(turn), np.cos(turn)], axis=1))
    second_table = np.concatenate(rows, axis=0)

    def halves(table):
        high = table.astype(ml_dtypes.bfloat16)
        return high, (table - high.astype(np.float64)).astype(ml_dtypes.bfloat16)

    first_table = np.concatenate(halves(first_table), axis=1)
    second_table = np.concatenate(halves(second_table), axis=0)
    return first_table, twist_table.astype(np.float32), second_table


def fused_kernel(
    S, T, norm_scale,
    samples_hbm, delays_hbm, fringe_hbm, first_hbm, twist_hbm, second_hbm,
    out_ref,
    flat, delays_ref, fringe_ref, first_ref, twist_ref, second_ref,
    signal, head, next_head, tail, outgoing, incoming, pieces, landed,
    load_sems, halo_sems, send_sem, recv_sem, last_sems, wave_sem, ready_sems,
):
    f32, bf16 = jnp.float32, jnp.bfloat16
    band = lax.axis_index("band")
    s_me = lax.axis_index("stn")
    t_me = lax.axis_index("tm")
    rows_chunk = CHUNK * 64
    chunks = signal.shape[0] // rows_chunk
    halo_rows = DMAX // LANES
    tail_start = (chunks - 1) * rows_chunk

    half = flat.shape[1] // 2
    loads = [
        pltpu.make_async_copy(source, target, load_sems.at[index])
        for index, (source, target) in enumerate(
            [
                (samples_hbm.at[:, pl.ds(0, half)], flat.at[:, pl.ds(0, half)]),
                (delays_hbm, delays_ref),
                (first_hbm, first_ref),
                (fringe_hbm, fringe_ref),
                (twist_hbm, twist_ref),
                (second_hbm, second_ref),
                (samples_hbm.at[:, pl.ds(half, half)], flat.at[:, pl.ds(half, half)]),
            ]
        )
    ]
    for load in loads:
        load.start()

    barrier = pltpu.get_barrier_semaphore()

    def tell(sem, s_to, t_to):
        pl.semaphore_signal(sem, inc=1, device_id=(band, s_to, t_to), device_id_type=MESH)

    for dt in range(1, T):
        tell(barrier, s_me, lax.rem(t_me + dt, T))

    @pl.when(s_me > 0)
    def _():
        tell(barrier, s_me - 1, t_me)

    @pl.when(s_me < S - 1)
    def _():
        tell(barrier, s_me + 1, t_me)

    def greet(station):
        pl.semaphore_wait(barrier, T - 1 + int(station > 0) + int(station < S - 1))
        if station > 0:
            pl.semaphore_wait(wave_sem, 1)
        if station < S - 1:
            tell(wave_sem, station + 1, t_me)
        for lower in range(station):
            tell(ready_sems.at[station], lower, t_me)

    @pl.when(s_me == S - 1)
    def _():
        greet(S - 1)

    tail[pl.ds(rows_chunk + halo_rows, 8), :] = jnp.zeros((8, LANES), f32)

    @pl.when(t_me == T - 1)
    def _():
        next_head[...] = jnp.zeros_like(next_head)

    def halo_copy():
        return pltpu.make_async_remote_copy(
            src_ref=head,
            dst_ref=next_head,
            send_sem=halo_sems.at[0],
            recv_sem=halo_sems.at[1],
            device_id=(band, s_me, lax.rem(t_me + T - 1, T)),
            device_id_type=MESH,
        )

    def lay_out(first_row, row_count):
        for row in range(first_row, first_row + row_count, 64):
            part = flat[:, pl.ds(row * LANES, 64 * LANES)].astype(f32).reshape(64, LANES)
            signal[pl.ds(row, 64), :] = part
            if row >= tail_start:
                tail[pl.ds(row - tail_start, 64), :] = part

    loads[0].wait()
    lay_out(0, 2 * rows_chunk)
    head[...] = signal[pl.ds(0, halo_rows), :].astype(bf16)

    @pl.when((s_me == S - 1) & (t_me > 0))
    def _():
        halo_copy().start()

    loads[1].wait()
    loads[2].wait()
    loads[3].wait()
    delay = delays_ref[0, 0]
    delay_rows = delay // LANES
    delay_lanes = delay - delay_rows * LANES
    lane_from = lax.broadcasted_iota(jnp.int32, (2 * LANES, LANES), 0)
    lane_to = lax.broadcasted_iota(jnp.int32, (2 * LANES, LANES), 1)
    shift = jnp.where(lane_from == lane_to + delay_lanes, 1.0, 0.0).astype(bf16)

    phase = fringe_ref[...].astype(f32) * (2.0 * math.pi / 65536.0)
    cos_fringe = jnp.cos(phase)
    sin_fringe = jnp.sin(phase)

    def chunk_spectra(c):
        source, start = (tail, 0) if c == chunks - 1 else (signal, c * rows_chunk)
        here = source[pl.ds(delay_rows + start, rows_chunk), :].astype(bf16)
        after = source[pl.ds(delay_rows + (start + 1), rows_chunk), :].astype(bf16)
        aligned = jnp.dot(
            jnp.concatenate([here, after], axis=1), shift, preferred_element_type=f32
        ).astype(bf16)
        frames = [aligned[64 * f : 64 * (f + 1)] for f in range(CHUNK)]
        side = jnp.concatenate(frames, axis=1)
        first = jnp.dot(
            first_ref[...], jnp.concatenate([side, side], axis=0), preferred_element_type=f32
        )
        twisted = []
        for f in range(CHUNK):
            at = c * CHUNK + f
            cos_f = cos_fringe[:, at : at + 1]
            sin_f = sin_fringe[:, at : at + 1]
            twist_real = twist_ref[0] * cos_f + twist_ref[1] * sin_f
            twist_imag = twist_ref[1] * cos_f - twist_ref[0] * sin_f
            real = first[:64, LANES * f : LANES * (f + 1)]
            imag = first[64:, LANES * f : LANES * (f + 1)]
            twisted.append(
                jnp.concatenate(
                    [
                        real * twist_real - imag * twist_imag,
                        real * twist_imag + imag * twist_real,
                    ],
                    axis=1,
                )
            )
        twisted = jnp.concatenate(twisted, axis=0)
        high = twisted.astype(bf16)
        low = (twisted - high.astype(f32)).astype(bf16)
        across = (((1,), (1,)), ((), ()))
        both = lax.dot_general(second_ref[...], high, across, preferred_element_type=f32)
        small = lax.dot_general(second_ref[:LANES], low, across, preferred_element_type=f32)
        spectra = both[:LANES] + (both[LANES:] + small)
        outgoing[:, c] = jnp.concatenate(
            [
                spectra[:, :LANES].reshape(S * T, 8, LANES),
                spectra[:, LANES:].reshape(S * T, 8, LANES),
            ],
            axis=1,
        ).astype(bf16)

    def send(first_chunk, chunk_count, s_to, dt):
        t_to = lax.rem(t_me + dt, T)
        part = pl.ds(first_chunk, chunk_count)
        pltpu.make_async_remote_copy(
            src_ref=outgoing.at[t_to * S + s_to, part],
            dst_ref=incoming.at[s_me * T + dt, part],
            send_sem=send_sem,
            recv_sem=recv_sem,
            device_id=(band, s_to, t_to),
            device_id_type=MESH,
        ).start()

    for c in range(chunks):
        if c == 0:
            loads[4].wait()
            loads[5].wait()
        elif c == 1:
            loads[6].wait()
            lay_out(2 * rows_chunk, rows_chunk)
        elif c == 2:
            lay_out(3 * rows_chunk, rows_chunk)
        else:

            @pl.when(t_me < T - 1)
            def _():
                halo_copy().wait_recv()

            tail[pl.ds(rows_chunk, halo_rows), :] = next_head[...].astype(f32)

        chunk_spectra(c)
        if c == 0:
            for station in range(S - 1):

                @pl.when(s_me == station)
                def _():
                    greet(station)

            @pl.when((s_me < S - 1) & (t_me > 0))
            def _():
                halo_copy().start()

        for lower in range(S - 1):

            @pl.when(lower < s_me)
            def _():
                for dt in range(T):
                    send(c, 1, lower, dt)

        for dt in range(1, T):
            send(c, 1, s_me, dt)
        incoming[s_me * T, c] = outgoing[t_me * S + s_me, c]

    for upper in range(1, S):

        @pl.when(upper > s_me)
        def _():
            pl.semaphore_wait(ready_sems.at[upper], 1)
            for dt in range(T):
                send(0, chunks, upper, dt)

    pairs = [(i, j) for i in range(S) for j in range(i, S)]
    even = {pair: jnp.zeros((8, LANES), f32) for pair in pairs}
    odd = {pair: jnp.zeros((8, LANES), f32) for pair in pairs if pair[0] != pair[1]}
    others = incoming.at[pl.ds(0, S * T - 1)]
    pltpu.make_async_copy(others, others, recv_sem).wait()
    for c in range(chunks):
        for dt in range(T):
            tiles = [incoming[s * T + dt, c].astype(f32) for s in range(S)]
            for top in (0, 8):
                part = [tile[top : top + 8] for tile in tiles]
                turned = [None] + [pltpu.roll(p, 4, 0) for p in part[1:]]
                for i, j in pairs:
                    even[i, j] += part[i] * part[j]
                    if i != j:
                        odd[i, j] += part[i] * turned[j]

    left = lax.broadcasted_iota(jnp.int32, (8, LANES), 1) < 64

    def settle(total, sign):
        total = total + pltpu.roll(total, 64, 1)
        total = (pltpu.roll(total, 4, 0) + sign * total) * norm_scale
        return jnp.where(left, total, pltpu.roll(total, 6, 0))

    def put(i, row, value):
        pieces[i, pl.ds(row, 1), pl.ds(0, LANES)] = value[0:1]
        pieces[i, pl.ds(row, 1), pl.ds(LANES, LANES)] = value[1:2]

    for i, j in pairs:
        real = settle(even[i, j], 1.0)
        put(i, j, real)
        if i == j:
            put(i, S + i, jnp.zeros_like(real))
        else:
            put(j, i, real)
            imag = settle(odd[i, j], -1.0)
            put(i, S + j, imag)
            put(j, S + i, -imag)

    def last_copy(ds):
        s_to = lax.rem(s_me + ds, S)
        return pltpu.make_async_remote_copy(
            src_ref=pieces.at[s_to],
            dst_ref=landed.at[s_me],
            send_sem=last_sems.at[0],
            recv_sem=last_sems.at[1],
            device_id=(band, s_to, t_me),
            device_id_type=MESH,
        )

    for ds in (2, 3, 1):
        last_copy(ds).start()
    landed[s_me] = pieces[s_me]
    others = landed.at[pl.ds(0, S - 1)]
    pltpu.make_async_copy(others, others, last_sems.at[1]).wait()
    for s in range(S):
        out_ref[:, pl.ds(s * 2 * LANES, 2 * LANES)] = landed[s]

    pltpu.make_async_copy(others, others, last_sems.at[0]).wait()
    sent = outgoing.at[pl.ds(0, S * T - 1)]
    pltpu.make_async_copy(sent, sent, send_sem).wait()

    @pl.when(t_me > 0)
    def _():
        halo_copy().wait_send()


def fused_on_device(stn_count, tm_count, samples, delays, fringe):
    length = samples.shape[1]
    rows = length // LANES
    chunks = rows // (CHUNK * 64)
    blocks = stn_count * tm_count
    norm_scale = 1.0 / math.sqrt(length // SPAN * tm_count)
    tables = spectrum_tables(stn_count, tm_count)
    operands = [samples, delays, fringe] + [jnp.asarray(table) for table in tables]
    out = pl.pallas_call(
        functools.partial(fused_kernel, stn_count, tm_count, norm_scale),
        out_shape=jax.ShapeDtypeStruct((2 * stn_count, 1024), jnp.float32),
        in_specs=[pl.BlockSpec(memory_space=pltpu.HBM)] * len(operands),
        out_specs=pl.BlockSpec(memory_space=pltpu.VMEM),
        scratch_shapes=[
            pltpu.VMEM(samples.shape, samples.dtype),
            pltpu.SMEM(delays.shape, delays.dtype),
        ]
        + [pltpu.VMEM(operand.shape, operand.dtype) for operand in operands[2:]]
        + [
            pltpu.VMEM((rows, LANES), jnp.float32),
            pltpu.VMEM((DMAX // LANES, LANES), jnp.bfloat16),
            pltpu.VMEM((DMAX // LANES, LANES), jnp.bfloat16),
            pltpu.VMEM((CHUNK * 64 + DMAX // LANES + 8, LANES), jnp.float32),
            pltpu.VMEM((blocks, chunks, 16, LANES), jnp.bfloat16),
            pltpu.VMEM((blocks, chunks, 16, LANES), jnp.bfloat16),
            pltpu.VMEM((stn_count, 2 * stn_count, 2 * LANES), jnp.float32),
            pltpu.VMEM((stn_count, 2 * stn_count, 2 * LANES), jnp.float32),
            pltpu.SemaphoreType.DMA((7,)),
            pltpu.SemaphoreType.DMA((2,)),
            pltpu.SemaphoreType.DMA,
            pltpu.SemaphoreType.DMA,
            pltpu.SemaphoreType.DMA((2,)),
            pltpu.SemaphoreType.REGULAR,
            pltpu.SemaphoreType.REGULAR((stn_count,)),
        ],
        compiler_params=pltpu.CompilerParams(
            collective_id=0, has_side_effects=True, vmem_limit_bytes=60 << 20
        ),
        name="correlate",
    )(*operands)
    return out.reshape(2, 1, stn_count, 1024)


def solution(mesh):
    stn_count, tm_count = mesh.shape["stn"], mesh.shape["tm"]
    body = on_device
    if (stn_count, tm_count) == (4, 4):
        body = functools.partial(fused_on_device, stn_count, tm_count)
    return jax.shard_map(
        body,
        mesh=mesh,
        in_specs=(P(("band", "stn"), "tm"), P("stn", "tm"), P(("band", "stn"), "tm")),
        out_specs=P(None, ("band", "stn"), None, "tm"),
        check_vma=False,
    )
```

```python
import functools
import math

import jax
import jax.numpy as jnp
import ml_dtypes
import numpy as np
from jax import lax
from jax.experimental import pallas as pl
from jax.experimental.pallas import tpu as pltpu
from jax.sharding import PartitionSpec as P

MESH = pl.DeviceIdType.MESH
SPAN = 8192
DMAX = 24576


def shifted(block, axis, distance):
    devices = range(lax.axis_size(axis))
    route = [(i - distance, i) for i in devices if i - distance in devices]
    return lax.ppermute(block, axis, route)


def passed_along(value, axis, by):
    size = lax.axis_size(axis)
    return lax.ppermute(value, axis, [(i, (i + by) % size) for i in range(size)])


def dft_tables():
    first_index = jnp.arange(64, dtype=jnp.int32)
    second_index = jnp.arange(128, dtype=jnp.int32)
    first_phase = (
        2.0 * jnp.pi * (first_index[:, None] * first_index[None, :] % 64).astype(jnp.float32) / 64.0
    )
    twist_phase = (
        2.0
        * jnp.pi
        * (first_index[:, None] * second_index[None, :] % 8192).astype(jnp.float32)
        / 8192.0
    )
    second_phase = (
        2.0
        * jnp.pi
        * (second_index[:, None] * first_index[None, :] % 128).astype(jnp.float32)
        / 128.0
    )
    return (first_phase, twist_phase, second_phase)


def spectrum(aligned, turn_table):
    stations, frames, span = aligned.shape
    first_phase, twist_phase, second_phase = dft_tables()
    high = lax.Precision.HIGHEST
    signal = aligned.astype(jnp.float32).reshape(stations, frames, 64, 128)
    first_real = jnp.einsum("sfab,ak->sfkb", signal, jnp.cos(first_phase), precision=high)
    first_imag = -jnp.einsum("sfab,ak->sfkb", signal, jnp.sin(first_phase), precision=high)
    cos_twist = jnp.cos(twist_phase)
    sin_twist = jnp.sin(twist_phase)
    twist_real = first_real * cos_twist + first_imag * sin_twist
    twist_imag = first_imag * cos_twist - first_real * sin_twist
    cos_second = jnp.cos(second_phase)
    sin_second = jnp.sin(second_phase)
    out_real = jnp.einsum("sfkb,bq->sfqk", twist_real, cos_second, precision=high) + jnp.einsum(
        "sfkb,bq->sfqk", twist_imag, sin_second, precision=high
    )
    out_imag = jnp.einsum("sfkb,bq->sfqk", twist_imag, cos_second, precision=high) - jnp.einsum(
        "sfkb,bq->sfqk", twist_real, sin_second, precision=high
    )
    norm_factor = 1.0 / jnp.sqrt(jnp.float32(span))
    out_real = out_real.reshape(stations, frames, span // 2) * norm_factor
    out_imag = out_imag.reshape(stations, frames, span // 2) * norm_factor
    phase_angle = (2.0 * jnp.pi * turn_table.astype(jnp.float32) / 65536.0)[:, :, None]
    cos_fringe = jnp.cos(phase_angle)
    sin_fringe = jnp.sin(phase_angle)
    rotated_real = out_real * cos_fringe + out_imag * sin_fringe
    rotated_imag = out_imag * cos_fringe - out_real * sin_fringe
    return jnp.stack([rotated_real, rotated_imag]).astype(jnp.bfloat16)


def cross(left_spec, right_spec):
    f32 = jnp.float32
    real_part = jnp.einsum(
        "afk,bfk->abk", left_spec[0], right_spec[0], preferred_element_type=f32
    ) + jnp.einsum("afk,bfk->abk", left_spec[1], right_spec[1], preferred_element_type=f32)
    imag_part = jnp.einsum(
        "afk,bfk->abk", left_spec[1], right_spec[0], preferred_element_type=f32
    ) - jnp.einsum("afk,bfk->abk", left_spec[0], right_spec[1], preferred_element_type=f32)
    return jnp.stack([real_part, imag_part])


def place(current_totals, block_term, first_station):
    current = lax.dynamic_slice_in_dim(current_totals, first_station, block_term.shape[2], 2)
    return lax.dynamic_update_slice_in_dim(current_totals, current + block_term, first_station, 2)


def on_device(samples, delays, fringe):
    stn_here, length = samples.shape
    frames_here = length // SPAN
    next_head = shifted(samples[:, :DMAX], "tm", -1)
    joined = jnp.concatenate([samples, next_head], axis=1)

    def take(sample_row, shift_by):
        return lax.dynamic_slice_in_dim(sample_row, shift_by, length)

    aligned = jax.vmap(take)(joined, delays[:, 0]).reshape(stn_here, frames_here, SPAN)
    own_spectra = spectrum(aligned, fringe)
    time_count = lax.axis_size("tm")
    channels_now = own_spectra.shape[3]
    cycle_size = lax.axis_size("stn")
    position = lax.axis_index("stn")
    totals = jnp.zeros((2, stn_here, stn_here * cycle_size, channels_now), jnp.float32)
    totals = place(totals, cross(own_spectra, own_spectra), position * stn_here)

    def turn_one(turn_index, state_tuple):
        current_totals, travel = state_tuple
        travel = passed_along(travel, "stn", 1)
        owner_index = (position - turn_index) % cycle_size
        current_totals = place(current_totals, cross(own_spectra, travel), owner_index * stn_here)
        return (current_totals, travel)

    totals, travel_end = lax.fori_loop(1, cycle_size, turn_one, (totals, own_spectra))
    norm_scale = 1.0 / jnp.sqrt(jnp.float32(frames_here * time_count))
    return lax.psum_scatter(totals * norm_scale, "tm", scatter_dimension=3, tiled=True)


LANES = 128
CHUNK = 4
GROUPS = ((0, 2), (3, 3))


def spectrum_tables(stn_count, tm_count):
    first = np.arange(64)
    second = np.arange(LANES)
    turn = 2.0 * np.pi * (first[:, None] * first[None, :] % 64) / 64.0
    first_table = np.concatenate([np.cos(turn), -np.sin(turn)], axis=0)
    twist = 2.0 * np.pi * (first[:, None] * second[None, :]) / SPAN
    twist_table = np.stack([np.cos(twist), -np.sin(twist)]) / np.sqrt(SPAN)
    rows = []
    for block in range(stn_count * tm_count):
        q = block * 4 + np.array([0, 2, 1, 3])
        turn = 2.0 * np.pi * (q[:, None] * second[None, :] % LANES) / LANES
        rows.append(np.concatenate([np.cos(turn), np.sin(turn)], axis=1))
        rows.append(np.concatenate([-np.sin(turn), np.cos(turn)], axis=1))
    second_table = np.concatenate(rows, axis=0)

    def halves(table):
        high = table.astype(ml_dtypes.bfloat16)
        return high, (table - high.astype(np.float64)).astype(ml_dtypes.bfloat16)

    first_table = np.concatenate(halves(first_table), axis=1)
    second_table = np.concatenate(halves(second_table), axis=0)
    return first_table, twist_table.astype(np.float32), second_table


def fused_kernel(
    S, T, norm_scale,
    samples_hbm, delays_hbm, fringe_hbm, first_hbm, twist_hbm, second_hbm,
    out_ref,
    flat, delays_ref, fringe_ref, first_ref, twist_ref, second_ref,
    signal, head, next_head, tail, outgoing, incoming, pieces, landed,
    load_sems, halo_sems, send_sem, recv_sems, last_sems,
):
    f32, bf16 = jnp.float32, jnp.bfloat16
    band = lax.axis_index("band")
    s_me = lax.axis_index("stn")
    t_me = lax.axis_index("tm")
    partners = [(ds, dt) for ds in (1, 2, 3, 0) for dt in range(T) if (ds, dt) != (0, 0)]
    late = s_me == S - 1
    rows_chunk = CHUNK * 64
    chunks = signal.shape[0] // rows_chunk
    halo_rows = DMAX // LANES
    tail_start = (chunks - 1) * rows_chunk

    def partner(ds, dt):
        if ds == 0:
            return s_me, lax.rem(t_me + dt, T)
        upward = ds - 1 + (s_me <= ds - 1).astype(jnp.int32)
        downward = S - ds - (S - 1 - s_me <= ds - 1).astype(jnp.int32)
        return lax.select(s_me >= S // 2, upward, downward), lax.rem(t_me + dt, T)

    half = flat.shape[1] // 2
    loads = [
        pltpu.make_async_copy(source, target, load_sems.at[index])
        for index, (source, target) in enumerate(
            [
                (samples_hbm.at[:, pl.ds(0, half)], flat.at[:, pl.ds(0, half)]),
                (delays_hbm, delays_ref),
                (first_hbm, first_ref),
                (fringe_hbm, fringe_ref),
                (twist_hbm, twist_ref),
                (second_hbm, second_ref),
                (samples_hbm.at[:, pl.ds(half, half)], flat.at[:, pl.ds(half, half)]),
            ]
        )
    ]
    for load in loads:
        load.start()

    barrier = pltpu.get_barrier_semaphore()
    for ds, dt in partners:
        s_to, t_to = partner(ds, dt)
        pl.semaphore_signal(barrier, inc=1, device_id=(band, s_to, t_to), device_id_type=MESH)

    tail[pl.ds(rows_chunk + halo_rows, 8), :] = jnp.zeros((8, LANES), f32)

    @pl.when(t_me == T - 1)
    def _():
        next_head[...] = jnp.zeros_like(next_head)

    def lay_out(first_row, row_count):
        for row in range(first_row, first_row + row_count, 64):
            part = flat[:, pl.ds(row * LANES, 64 * LANES)].astype(f32).reshape(64, LANES)
            signal[pl.ds(row, 64), :] = part
            if row >= tail_start:
                tail[pl.ds(row - tail_start, 64), :] = part

    loads[0].wait()
    lay_out(0, 2 * rows_chunk)
    head[...] = signal[pl.ds(0, halo_rows), :].astype(bf16)
    loads[1].wait()
    loads[2].wait()
    loads[3].wait()
    delay = delays_ref[0, 0]
    delay_rows = delay // LANES
    delay_lanes = delay - delay_rows * LANES
    lane_from = lax.broadcasted_iota(jnp.int32, (2 * LANES, LANES), 0)
    lane_to = lax.broadcasted_iota(jnp.int32, (2 * LANES, LANES), 1)
    shift = jnp.where(lane_from == lane_to + delay_lanes, 1.0, 0.0).astype(bf16)

    phase = fringe_ref[...].astype(f32) * (2.0 * math.pi / 65536.0)
    cos_fringe = jnp.cos(phase)
    sin_fringe = jnp.sin(phase)

    def chunk_spectra(c):
        source, start = (tail, 0) if c == chunks - 1 else (signal, c * rows_chunk)
        here = source[pl.ds(delay_rows + start, rows_chunk), :].astype(bf16)
        after = source[pl.ds(delay_rows + (start + 1), rows_chunk), :].astype(bf16)
        aligned = jnp.dot(
            jnp.concatenate([here, after], axis=1), shift, preferred_element_type=f32
        ).astype(bf16)
        frames = [aligned[64 * f : 64 * (f + 1)] for f in range(CHUNK)]
        side = jnp.concatenate(frames, axis=1)
        first = jnp.dot(
            first_ref[...], jnp.concatenate([side, side], axis=0), preferred_element_type=f32
        )
        twisted = []
        for f in range(CHUNK):
            at = c * CHUNK + f
            cos_f = cos_fringe[:, at : at + 1]
            sin_f = sin_fringe[:, at : at + 1]
            twist_real = twist_ref[0] * cos_f + twist_ref[1] * sin_f
            twist_imag = twist_ref[1] * cos_f - twist_ref[0] * sin_f
            real = first[:64, LANES * f : LANES * (f + 1)]
            imag = first[64:, LANES * f : LANES * (f + 1)]
            twisted.append(
                jnp.concatenate(
                    [
                        real * twist_real - imag * twist_imag,
                        real * twist_imag + imag * twist_real,
                    ],
                    axis=1,
                )
            )
        twisted = jnp.concatenate(twisted, axis=0)
        high = twisted.astype(bf16)
        low = (twisted - high.astype(f32)).astype(bf16)
        across = (((1,), (1,)), ((), ()))
        both = lax.dot_general(second_ref[...], high, across, preferred_element_type=f32)
        small = lax.dot_general(second_ref[:LANES], low, across, preferred_element_type=f32)
        spectra = both[:LANES] + (both[LANES:] + small)
        outgoing[:, c] = jnp.concatenate(
            [
                spectra[:, :LANES].reshape(S * T, 8, LANES),
                spectra[:, LANES:].reshape(S * T, 8, LANES),
            ],
            axis=1,
        ).astype(bf16)

    def spectra_copy(group, first_chunk, last_chunk, ds, dt):
        s_to, t_to = partner(ds, dt)
        part = pl.ds(first_chunk, last_chunk + 1 - first_chunk)
        return pltpu.make_async_remote_copy(
            src_ref=outgoing.at[t_to * S + s_to, part],
            dst_ref=incoming.at[s_me * T + dt, part],
            send_sem=send_sem,
            recv_sem=recv_sems.at[group],
            device_id=(band, s_to, t_to),
            device_id_type=MESH,
        )

    def all_arrived(group):
        first_chunk, last_chunk = GROUPS[group]
        part = incoming.at[pl.ds(0, S * T - 1), pl.ds(first_chunk, last_chunk + 1 - first_chunk)]
        pltpu.make_async_copy(part, part, recv_sems.at[group]).wait()

    def halo_copy():
        return pltpu.make_async_remote_copy(
            src_ref=head,
            dst_ref=next_head,
            send_sem=halo_sems.at[0],
            recv_sem=halo_sems.at[1],
            device_id=(band, s_me, lax.rem(t_me + T - 1, T)),
            device_id_type=MESH,
        )

    for c in range(chunks):
        if c == 0:
            loads[4].wait()
            loads[5].wait()
        elif c == 1:
            loads[6].wait()
            lay_out(2 * rows_chunk, rows_chunk)
        elif c == 2:
            lay_out(3 * rows_chunk, rows_chunk)
        else:

            @pl.when(t_me < T - 1)
            def _():
                halo_copy().wait_recv()

            tail[pl.ds(rows_chunk, halo_rows), :] = next_head[...].astype(f32)

        chunk_spectra(c)
        def open_exchange():
            pl.semaphore_wait(barrier, len(partners))

            @pl.when(t_me > 0)
            def _():
                halo_copy().start()

        if c == 0:
            pl.when(late)(open_exchange)
        if c == GROUPS[0][1]:
            pl.when(jnp.logical_not(late))(open_exchange)

        if c <= GROUPS[0][1]:

            @pl.when(late)
            def _():
                for ds, dt in partners:
                    spectra_copy(0, c, c, ds, dt).start()

        for group, (first_chunk, last_chunk) in enumerate(GROUPS):
            if last_chunk == c:

                @pl.when(jnp.logical_not(late) if group == 0 else True)
                def _():
                    for ds, dt in partners:
                        spectra_copy(group, first_chunk, last_chunk, ds, dt).start()

        incoming[s_me * T, c] = outgoing[t_me * S + s_me, c]

    pairs = [(i, j) for i in range(S) for j in range(i, S)]
    even = {pair: jnp.zeros((8, LANES), f32) for pair in pairs}
    odd = {pair: jnp.zeros((8, LANES), f32) for pair in pairs if pair[0] != pair[1]}
    for group, (first_chunk, last_chunk) in enumerate(GROUPS):
        all_arrived(group)
        for dt, c in [(dt, c) for dt in range(T) for c in range(first_chunk, last_chunk + 1)]:
            tiles = [incoming[s * T + dt, c].astype(f32) for s in range(S)]
            for top in (0, 8):
                part = [tile[top : top + 8] for tile in tiles]
                turned = [None] + [pltpu.roll(p, 4, 0) for p in part[1:]]
                for i, j in pairs:
                    even[i, j] += part[i] * part[j]
                    if i != j:
                        odd[i, j] += part[i] * turned[j]

    left = lax.broadcasted_iota(jnp.int32, (8, LANES), 1) < 64

    def settle(total, sign):
        total = total + pltpu.roll(total, 64, 1)
        total = (pltpu.roll(total, 4, 0) + sign * total) * norm_scale
        return jnp.where(left, total, pltpu.roll(total, 6, 0))

    def put(i, row, value):
        pieces[i, pl.ds(row, 1), pl.ds(0, LANES)] = value[0:1]
        pieces[i, pl.ds(row, 1), pl.ds(LANES, LANES)] = value[1:2]

    for i, j in pairs:
        real = settle(even[i, j], 1.0)
        put(i, j, real)
        if i == j:
            put(i, S + i, jnp.zeros_like(real))
        else:
            put(j, i, real)
            imag = settle(odd[i, j], -1.0)
            put(i, S + j, imag)
            put(j, S + i, -imag)

    def last_copy(ds):
        s_to, _ = partner(ds, 0)
        return pltpu.make_async_remote_copy(
            src_ref=pieces.at[s_to],
            dst_ref=landed.at[s_me],
            send_sem=last_sems.at[0],
            recv_sem=last_sems.at[1],
            device_id=(band, s_to, t_me),
            device_id_type=MESH,
        )

    for ds in (1, 2, 3):
        last_copy(ds).start()
    landed[s_me] = pieces[s_me]
    others = landed.at[pl.ds(0, S - 1)]
    pltpu.make_async_copy(others, others, last_sems.at[1]).wait()
    for s in range(S):
        out_ref[:, pl.ds(s * 2 * LANES, 2 * LANES)] = landed[s]

    pltpu.make_async_copy(others, others, last_sems.at[0]).wait()
    sent = outgoing.at[pl.ds(0, S * T - 1)]
    pltpu.make_async_copy(sent, sent, send_sem).wait()

    @pl.when(t_me > 0)
    def _():
        halo_copy().wait_send()


def fused_on_device(stn_count, tm_count, samples, delays, fringe):
    length = samples.shape[1]
    rows = length // LANES
    chunks = rows // (CHUNK * 64)
    blocks = stn_count * tm_count
    norm_scale = 1.0 / math.sqrt(length // SPAN * tm_count)
    tables = spectrum_tables(stn_count, tm_count)
    operands = [samples, delays, fringe] + [jnp.asarray(table) for table in tables]
    out = pl.pallas_call(
        functools.partial(fused_kernel, stn_count, tm_count, norm_scale),
        out_shape=pltpu.VMEM((2 * stn_count, 1024), jnp.float32),
        in_specs=[pl.BlockSpec(memory_space=pltpu.HBM)] * len(operands),
        out_specs=pl.BlockSpec(memory_space=pltpu.VMEM),
        scratch_shapes=[
            pltpu.VMEM(samples.shape, samples.dtype),
            pltpu.SMEM(delays.shape, delays.dtype),
        ]
        + [pltpu.VMEM(operand.shape, operand.dtype) for operand in operands[2:]]
        + [
            pltpu.VMEM((rows, LANES), jnp.float32),
            pltpu.VMEM((DMAX // LANES, LANES), jnp.bfloat16),
            pltpu.VMEM((DMAX // LANES, LANES), jnp.bfloat16),
            pltpu.VMEM((CHUNK * 64 + DMAX // LANES + 8, LANES), jnp.float32),
            pltpu.VMEM((blocks, chunks, 16, LANES), jnp.bfloat16),
            pltpu.VMEM((blocks, chunks, 16, LANES), jnp.bfloat16),
            pltpu.VMEM((stn_count, 2 * stn_count, 2 * LANES), jnp.float32),
            pltpu.VMEM((stn_count, 2 * stn_count, 2 * LANES), jnp.float32),
            pltpu.SemaphoreType.DMA((7,)),
            pltpu.SemaphoreType.DMA((2,)),
            pltpu.SemaphoreType.DMA,
            pltpu.SemaphoreType.DMA((len(GROUPS),)),
            pltpu.SemaphoreType.DMA((2,)),
        ],
        compiler_params=pltpu.CompilerParams(
            collective_id=0, has_side_effects=True, vmem_limit_bytes=60 << 20
        ),
        name="correlate",
    )(*operands)
    return out.reshape(2, 1, stn_count, 1024)


def solution(mesh):
    stn_count, tm_count = mesh.shape["stn"], mesh.shape["tm"]
    body = on_device
    if (stn_count, tm_count) == (4, 4):
        body = functools.partial(fused_on_device, stn_count, tm_count)
    return jax.shard_map(
        body,
        mesh=mesh,
        in_specs=(P(("band", "stn"), "tm"), P("stn", "tm"), P(("band", "stn"), "tm")),
        out_specs=P(None, ("band", "stn"), None, "tm"),
        check_vma=False,
    )
```

```python
import functools
import math

import jax
import jax.numpy as jnp
import ml_dtypes
import numpy as np
from jax import lax
from jax.experimental import pallas as pl
from jax.experimental.pallas import tpu as pltpu
from jax.sharding import PartitionSpec as P

MESH = pl.DeviceIdType.MESH
SPAN = 8192
DMAX = 24576


def shifted(block, axis, distance):
    devices = range(lax.axis_size(axis))
    route = [(i - distance, i) for i in devices if i - distance in devices]
    return lax.ppermute(block, axis, route)


def passed_along(value, axis, by):
    size = lax.axis_size(axis)
    return lax.ppermute(value, axis, [(i, (i + by) % size) for i in range(size)])


def dft_tables():
    first_index = jnp.arange(64, dtype=jnp.int32)
    second_index = jnp.arange(128, dtype=jnp.int32)
    first_phase = (
        2.0 * jnp.pi * (first_index[:, None] * first_index[None, :] % 64).astype(jnp.float32) / 64.0
    )
    twist_phase = (
        2.0
        * jnp.pi
        * (first_index[:, None] * second_index[None, :] % 8192).astype(jnp.float32)
        / 8192.0
    )
    second_phase = (
        2.0
        * jnp.pi
        * (second_index[:, None] * first_index[None, :] % 128).astype(jnp.float32)
        / 128.0
    )
    return (first_phase, twist_phase, second_phase)


def spectrum(aligned, turn_table):
    stations, frames, span = aligned.shape
    first_phase, twist_phase, second_phase = dft_tables()
    high = lax.Precision.HIGHEST
    signal = aligned.astype(jnp.float32).reshape(stations, frames, 64, 128)
    first_real = jnp.einsum("sfab,ak->sfkb", signal, jnp.cos(first_phase), precision=high)
    first_imag = -jnp.einsum("sfab,ak->sfkb", signal, jnp.sin(first_phase), precision=high)
    cos_twist = jnp.cos(twist_phase)
    sin_twist = jnp.sin(twist_phase)
    twist_real = first_real * cos_twist + first_imag * sin_twist
    twist_imag = first_imag * cos_twist - first_real * sin_twist
    cos_second = jnp.cos(second_phase)
    sin_second = jnp.sin(second_phase)
    out_real = jnp.einsum("sfkb,bq->sfqk", twist_real, cos_second, precision=high) + jnp.einsum(
        "sfkb,bq->sfqk", twist_imag, sin_second, precision=high
    )
    out_imag = jnp.einsum("sfkb,bq->sfqk", twist_imag, cos_second, precision=high) - jnp.einsum(
        "sfkb,bq->sfqk", twist_real, sin_second, precision=high
    )
    norm_factor = 1.0 / jnp.sqrt(jnp.float32(span))
    out_real = out_real.reshape(stations, frames, span // 2) * norm_factor
    out_imag = out_imag.reshape(stations, frames, span // 2) * norm_factor
    phase_angle = (2.0 * jnp.pi * turn_table.astype(jnp.float32) / 65536.0)[:, :, None]
    cos_fringe = jnp.cos(phase_angle)
    sin_fringe = jnp.sin(phase_angle)
    rotated_real = out_real * cos_fringe + out_imag * sin_fringe
    rotated_imag = out_imag * cos_fringe - out_real * sin_fringe
    return jnp.stack([rotated_real, rotated_imag]).astype(jnp.bfloat16)


def cross(left_spec, right_spec):
    f32 = jnp.float32
    real_part = jnp.einsum(
        "afk,bfk->abk", left_spec[0], right_spec[0], preferred_element_type=f32
    ) + jnp.einsum("afk,bfk->abk", left_spec[1], right_spec[1], preferred_element_type=f32)
    imag_part = jnp.einsum(
        "afk,bfk->abk", left_spec[1], right_spec[0], preferred_element_type=f32
    ) - jnp.einsum("afk,bfk->abk", left_spec[0], right_spec[1], preferred_element_type=f32)
    return jnp.stack([real_part, imag_part])


def place(current_totals, block_term, first_station):
    current = lax.dynamic_slice_in_dim(current_totals, first_station, block_term.shape[2], 2)
    return lax.dynamic_update_slice_in_dim(current_totals, current + block_term, first_station, 2)


def on_device(samples, delays, fringe):
    stn_here, length = samples.shape
    frames_here = length // SPAN
    next_head = shifted(samples[:, :DMAX], "tm", -1)
    joined = jnp.concatenate([samples, next_head], axis=1)

    def take(sample_row, shift_by):
        return lax.dynamic_slice_in_dim(sample_row, shift_by, length)

    aligned = jax.vmap(take)(joined, delays[:, 0]).reshape(stn_here, frames_here, SPAN)
    own_spectra = spectrum(aligned, fringe)
    time_count = lax.axis_size("tm")
    channels_now = own_spectra.shape[3]
    cycle_size = lax.axis_size("stn")
    position = lax.axis_index("stn")
    totals = jnp.zeros((2, stn_here, stn_here * cycle_size, channels_now), jnp.float32)
    totals = place(totals, cross(own_spectra, own_spectra), position * stn_here)

    def turn_one(turn_index, state_tuple):
        current_totals, travel = state_tuple
        travel = passed_along(travel, "stn", 1)
        owner_index = (position - turn_index) % cycle_size
        current_totals = place(current_totals, cross(own_spectra, travel), owner_index * stn_here)
        return (current_totals, travel)

    totals, travel_end = lax.fori_loop(1, cycle_size, turn_one, (totals, own_spectra))
    norm_scale = 1.0 / jnp.sqrt(jnp.float32(frames_here * time_count))
    return lax.psum_scatter(totals * norm_scale, "tm", scatter_dimension=3, tiled=True)


LANES = 128
CHUNK = 4
GROUPS = ((0, 2), (3, 3))


def spectrum_tables(stn_count, tm_count):
    first = np.arange(64)
    second = np.arange(LANES)
    turn = 2.0 * np.pi * (first[:, None] * first[None, :] % 64) / 64.0
    first_table = np.concatenate([np.cos(turn), -np.sin(turn)], axis=0)
    twist = 2.0 * np.pi * (first[:, None] * second[None, :]) / SPAN
    twist_table = np.stack([np.cos(twist), -np.sin(twist)]) / np.sqrt(SPAN)
    rows = []
    for block in range(stn_count * tm_count):
        q = block * 4 + np.array([0, 2, 1, 3])
        turn = 2.0 * np.pi * (q[:, None] * second[None, :] % LANES) / LANES
        rows.append(np.concatenate([np.cos(turn), np.sin(turn)], axis=1))
        rows.append(np.concatenate([-np.sin(turn), np.cos(turn)], axis=1))
    second_table = np.concatenate(rows, axis=0)

    def halves(table):
        high = table.astype(ml_dtypes.bfloat16)
        return high, (table - high.astype(np.float64)).astype(ml_dtypes.bfloat16)

    first_table = np.concatenate(halves(first_table), axis=1)
    second_table = np.concatenate(halves(second_table), axis=0)
    return first_table, twist_table.astype(np.float32), second_table


def fused_kernel(
    S, T, norm_scale,
    samples_hbm, delays_hbm, fringe_hbm, first_hbm, twist_hbm, second_hbm,
    out_ref,
    flat, delays_ref, fringe_ref, first_ref, twist_ref, second_ref,
    signal, head, next_head, tail, outgoing, incoming, pieces, landed,
    load_sems, halo_sems, send_sem, recv_sems, last_sems,
):
    f32, bf16 = jnp.float32, jnp.bfloat16
    band = lax.axis_index("band")
    s_me = lax.axis_index("stn")
    t_me = lax.axis_index("tm")
    partners = [(ds, dt) for ds in (1, 2, 3, 0) for dt in (2, 3, 0, 1) if (ds, dt) != (0, 0)]
    late = s_me == S - 1
    rows_chunk = CHUNK * 64
    chunks = signal.shape[0] // rows_chunk
    halo_rows = DMAX // LANES
    tail_start = (chunks - 1) * rows_chunk

    def partner(ds, dt):
        if ds == 0:
            return s_me, lax.rem(t_me + dt, T)
        upward = ds - 1 + (s_me <= ds - 1).astype(jnp.int32)
        downward = S - ds - (S - 1 - s_me <= ds - 1).astype(jnp.int32)
        return lax.select(s_me >= S // 2, upward, downward), lax.rem(t_me + dt, T)

    half = flat.shape[1] // 2
    loads = [
        pltpu.make_async_copy(source, target, load_sems.at[index])
        for index, (source, target) in enumerate(
            [
                (samples_hbm.at[:, pl.ds(0, half)], flat.at[:, pl.ds(0, half)]),
                (delays_hbm, delays_ref),
                (first_hbm, first_ref),
                (fringe_hbm, fringe_ref),
                (twist_hbm, twist_ref),
                (second_hbm, second_ref),
                (samples_hbm.at[:, pl.ds(half, half)], flat.at[:, pl.ds(half, half)]),
            ]
        )
    ]
    for load in loads:
        load.start()

    barrier = pltpu.get_barrier_semaphore()
    for ds, dt in partners:
        s_to, t_to = partner(ds, dt)
        pl.semaphore_signal(barrier, inc=1, device_id=(band, s_to, t_to), device_id_type=MESH)

    tail[pl.ds(rows_chunk + halo_rows, 8), :] = jnp.zeros((8, LANES), f32)

    @pl.when(t_me == T - 1)
    def _():
        next_head[...] = jnp.zeros_like(next_head)

    def lay_out(first_row, row_count):
        for row in range(first_row, first_row + row_count, 64):
            part = flat[:, pl.ds(row * LANES, 64 * LANES)].astype(f32).reshape(64, LANES)
            signal[pl.ds(row, 64), :] = part
            if row >= tail_start:
                tail[pl.ds(row - tail_start, 64), :] = part

    loads[0].wait()
    lay_out(0, 2 * rows_chunk)
    head[...] = signal[pl.ds(0, halo_rows), :].astype(bf16)
    loads[1].wait()
    loads[2].wait()
    loads[3].wait()
    delay = delays_ref[0, 0]
    delay_rows = delay // LANES
    delay_lanes = delay - delay_rows * LANES
    lane_from = lax.broadcasted_iota(jnp.int32, (2 * LANES, LANES), 0)
    lane_to = lax.broadcasted_iota(jnp.int32, (2 * LANES, LANES), 1)
    shift = jnp.where(lane_from == lane_to + delay_lanes, 1.0, 0.0).astype(bf16)

    phase = fringe_ref[...].astype(f32) * (2.0 * math.pi / 65536.0)
    cos_fringe = jnp.cos(phase)
    sin_fringe = jnp.sin(phase)

    def chunk_spectra(c):
        source, start = (tail, 0) if c == chunks - 1 else (signal, c * rows_chunk)
        here = source[pl.ds(delay_rows + start, rows_chunk), :].astype(bf16)
        after = source[pl.ds(delay_rows + (start + 1), rows_chunk), :].astype(bf16)
        aligned = jnp.dot(
            jnp.concatenate([here, after], axis=1), shift, preferred_element_type=f32
        ).astype(bf16)
        frames = [aligned[64 * f : 64 * (f + 1)] for f in range(CHUNK)]
        side = jnp.concatenate(frames, axis=1)
        first = jnp.dot(
            first_ref[...], jnp.concatenate([side, side], axis=0), preferred_element_type=f32
        )
        twisted = []
        for f in range(CHUNK):
            at = c * CHUNK + f
            cos_f = cos_fringe[:, at : at + 1]
            sin_f = sin_fringe[:, at : at + 1]
            twist_real = twist_ref[0] * cos_f + twist_ref[1] * sin_f
            twist_imag = twist_ref[1] * cos_f - twist_ref[0] * sin_f
            real = first[:64, LANES * f : LANES * (f + 1)]
            imag = first[64:, LANES * f : LANES * (f + 1)]
            twisted.append(
                jnp.concatenate(
                    [
                        real * twist_real - imag * twist_imag,
                        real * twist_imag + imag * twist_real,
                    ],
                    axis=1,
                )
            )
        twisted = jnp.concatenate(twisted, axis=0)
        high = twisted.astype(bf16)
        low = (twisted - high.astype(f32)).astype(bf16)
        across = (((1,), (1,)), ((), ()))
        both = lax.dot_general(second_ref[...], high, across, preferred_element_type=f32)
        small = lax.dot_general(second_ref[:LANES], low, across, preferred_element_type=f32)
        spectra = both[:LANES] + (both[LANES:] + small)
        outgoing[:, c] = jnp.concatenate(
            [
                spectra[:, :LANES].reshape(S * T, 8, LANES),
                spectra[:, LANES:].reshape(S * T, 8, LANES),
            ],
            axis=1,
        ).astype(bf16)

    def spectra_copy(group, first_chunk, last_chunk, ds, dt):
        s_to, t_to = partner(ds, dt)
        part = pl.ds(first_chunk, last_chunk + 1 - first_chunk)
        return pltpu.make_async_remote_copy(
            src_ref=outgoing.at[t_to * S + s_to, part],
            dst_ref=incoming.at[s_me * T + dt, part],
            send_sem=send_sem,
            recv_sem=recv_sems.at[group],
            device_id=(band, s_to, t_to),
            device_id_type=MESH,
        )

    def all_arrived(group):
        first_chunk, last_chunk = GROUPS[group]
        part = incoming.at[pl.ds(0, S * T - 1), pl.ds(first_chunk, last_chunk + 1 - first_chunk)]
        pltpu.make_async_copy(part, part, recv_sems.at[group]).wait()

    def halo_copy():
        return pltpu.make_async_remote_copy(
            src_ref=head,
            dst_ref=next_head,
            send_sem=halo_sems.at[0],
            recv_sem=halo_sems.at[1],
            device_id=(band, s_me, lax.rem(t_me + T - 1, T)),
            device_id_type=MESH,
        )

    for c in range(chunks):
        if c == 0:
            loads[4].wait()
            loads[5].wait()
        elif c == 1:
            loads[6].wait()
            lay_out(2 * rows_chunk, rows_chunk)
        elif c == 2:
            lay_out(3 * rows_chunk, rows_chunk)
        else:

            @pl.when(t_me < T - 1)
            def _():
                halo_copy().wait_recv()

            tail[pl.ds(rows_chunk, halo_rows), :] = next_head[...].astype(f32)

        chunk_spectra(c)
        def open_exchange():
            pl.semaphore_wait(barrier, len(partners))

            @pl.when(t_me > 0)
            def _():
                halo_copy().start()

        if c == 0:
            pl.when(late)(open_exchange)
        if c == GROUPS[0][1]:
            pl.when(jnp.logical_not(late))(open_exchange)

        if c <= GROUPS[0][1]:

            @pl.when(late)
            def _():
                for ds, dt in partners:
                    spectra_copy(0, c, c, ds, dt).start()

        for group, (first_chunk, last_chunk) in enumerate(GROUPS):
            if last_chunk == c:

                @pl.when(jnp.logical_not(late) if group == 0 else True)
                def _():
                    for ds, dt in partners:
                        spectra_copy(group, first_chunk, last_chunk, ds, dt).start()

        incoming[s_me * T, c] = outgoing[t_me * S + s_me, c]

    pairs = [(i, j) for i in range(S) for j in range(i, S)]
    even = {pair: jnp.zeros((8, LANES), f32) for pair in pairs}
    odd = {pair: jnp.zeros((8, LANES), f32) for pair in pairs if pair[0] != pair[1]}
    for group, (first_chunk, last_chunk) in enumerate(GROUPS):
        all_arrived(group)
        for dt, c in [(dt, c) for dt in range(T) for c in range(first_chunk, last_chunk + 1)]:
            tiles = [incoming[s * T + dt, c].astype(f32) for s in range(S)]
            for top in (0, 8):
                part = [tile[top : top + 8] for tile in tiles]
                turned = [None] + [pltpu.roll(p, 4, 0) for p in part[1:]]
                for i, j in pairs:
                    even[i, j] += part[i] * part[j]
                    if i != j:
                        odd[i, j] += part[i] * turned[j]

    left = lax.broadcasted_iota(jnp.int32, (8, LANES), 1) < 64

    def settle(total, sign):
        total = total + pltpu.roll(total, 64, 1)
        total = (pltpu.roll(total, 4, 0) + sign * total) * norm_scale
        return jnp.where(left, total, pltpu.roll(total, 6, 0))

    def put(i, row, value):
        pieces[i, pl.ds(row, 1), pl.ds(0, LANES)] = value[0:1]
        pieces[i, pl.ds(row, 1), pl.ds(LANES, LANES)] = value[1:2]

    for i, j in pairs:
        real = settle(even[i, j], 1.0)
        put(i, j, real)
        if i == j:
            put(i, S + i, jnp.zeros_like(real))
        else:
            put(j, i, real)
            imag = settle(odd[i, j], -1.0)
            put(i, S + j, imag)
            put(j, S + i, -imag)

    def last_copy(ds):
        s_to, _ = partner(ds, 0)
        return pltpu.make_async_remote_copy(
            src_ref=pieces.at[s_to],
            dst_ref=landed.at[s_me],
            send_sem=last_sems.at[0],
            recv_sem=last_sems.at[1],
            device_id=(band, s_to, t_me),
            device_id_type=MESH,
        )

    for ds in (1, 2, 3):
        last_copy(ds).start()
    landed[s_me] = pieces[s_me]
    others = landed.at[pl.ds(0, S - 1)]
    pltpu.make_async_copy(others, others, last_sems.at[1]).wait()
    for s in range(S):
        for part in range(2):
            out_ref[part, :, pl.ds(s * 2 * LANES, 2 * LANES)] = landed[s, S * part : S * part + S]

    pltpu.make_async_copy(others, others, last_sems.at[0]).wait()
    sent = outgoing.at[pl.ds(0, S * T - 1)]
    pltpu.make_async_copy(sent, sent, send_sem).wait()

    @pl.when(t_me > 0)
    def _():
        halo_copy().wait_send()


def fused_on_device(stn_count, tm_count, samples, delays, fringe):
    length = samples.shape[1]
    rows = length // LANES
    chunks = rows // (CHUNK * 64)
    blocks = stn_count * tm_count
    norm_scale = 1.0 / math.sqrt(length // SPAN * tm_count)
    tables = spectrum_tables(stn_count, tm_count)
    operands = [samples, delays, fringe] + [jnp.asarray(table) for table in tables]
    out = pl.pallas_call(
        functools.partial(fused_kernel, stn_count, tm_count, norm_scale),
        out_shape=pltpu.VMEM((2, stn_count, 1024), jnp.float32),
        in_specs=[pl.BlockSpec(memory_space=pltpu.HBM)] * len(operands),
        out_specs=pl.BlockSpec(memory_space=pltpu.VMEM),
        scratch_shapes=[
            pltpu.VMEM(samples.shape, samples.dtype),
            pltpu.SMEM(delays.shape, delays.dtype),
        ]
        + [pltpu.VMEM(operand.shape, operand.dtype) for operand in operands[2:]]
        + [
            pltpu.VMEM((rows, LANES), jnp.float32),
            pltpu.VMEM((DMAX // LANES, LANES), jnp.bfloat16),
            pltpu.VMEM((DMAX // LANES, LANES), jnp.bfloat16),
            pltpu.VMEM((CHUNK * 64 + DMAX // LANES + 8, LANES), jnp.float32),
            pltpu.VMEM((blocks, chunks, 16, LANES), jnp.bfloat16),
            pltpu.VMEM((blocks, chunks, 16, LANES), jnp.bfloat16),
            pltpu.VMEM((stn_count, 2 * stn_count, 2 * LANES), jnp.float32),
            pltpu.VMEM((stn_count, 2 * stn_count, 2 * LANES), jnp.float32),
            pltpu.SemaphoreType.DMA((7,)),
            pltpu.SemaphoreType.DMA((2,)),
            pltpu.SemaphoreType.DMA,
            pltpu.SemaphoreType.DMA((len(GROUPS),)),
            pltpu.SemaphoreType.DMA((2,)),
        ],
        compiler_params=pltpu.CompilerParams(
            collective_id=0, has_side_effects=True, vmem_limit_bytes=60 << 20
        ),
        name="correlate",
    )(*operands)
    return out[:, None]


def solution(mesh):
    stn_count, tm_count = mesh.shape["stn"], mesh.shape["tm"]
    body = on_device
    if (stn_count, tm_count) == (4, 4):
        body = functools.partial(fused_on_device, stn_count, tm_count)
    return jax.shard_map(
        body,
        mesh=mesh,
        in_specs=(P(("band", "stn"), "tm"), P("stn", "tm"), P(("band", "stn"), "tm")),
        out_specs=P(None, ("band", "stn"), None, "tm"),
        check_vma=False,
    )
```

```python
import functools
import math

import jax
import jax.numpy as jnp
import ml_dtypes
import numpy as np
from jax import lax
from jax.experimental import pallas as pl
from jax.experimental.pallas import tpu as pltpu
from jax.sharding import PartitionSpec as P

MESH = pl.DeviceIdType.MESH
SPAN = 8192
DMAX = 24576


def shifted(block, axis, distance):
    devices = range(lax.axis_size(axis))
    route = [(i - distance, i) for i in devices if i - distance in devices]
    return lax.ppermute(block, axis, route)


def passed_along(value, axis, by):
    size = lax.axis_size(axis)
    return lax.ppermute(value, axis, [(i, (i + by) % size) for i in range(size)])


def dft_tables():
    first_index = jnp.arange(64, dtype=jnp.int32)
    second_index = jnp.arange(128, dtype=jnp.int32)
    first_phase = (
        2.0 * jnp.pi * (first_index[:, None] * first_index[None, :] % 64).astype(jnp.float32) / 64.0
    )
    twist_phase = (
        2.0
        * jnp.pi
        * (first_index[:, None] * second_index[None, :] % 8192).astype(jnp.float32)
        / 8192.0
    )
    second_phase = (
        2.0
        * jnp.pi
        * (second_index[:, None] * first_index[None, :] % 128).astype(jnp.float32)
        / 128.0
    )
    return (first_phase, twist_phase, second_phase)


def spectrum(aligned, turn_table):
    stations, frames, span = aligned.shape
    first_phase, twist_phase, second_phase = dft_tables()
    high = lax.Precision.HIGHEST
    signal = aligned.astype(jnp.float32).reshape(stations, frames, 64, 128)
    first_real = jnp.einsum("sfab,ak->sfkb", signal, jnp.cos(first_phase), precision=high)
    first_imag = -jnp.einsum("sfab,ak->sfkb", signal, jnp.sin(first_phase), precision=high)
    cos_twist = jnp.cos(twist_phase)
    sin_twist = jnp.sin(twist_phase)
    twist_real = first_real * cos_twist + first_imag * sin_twist
    twist_imag = first_imag * cos_twist - first_real * sin_twist
    cos_second = jnp.cos(second_phase)
    sin_second = jnp.sin(second_phase)
    out_real = jnp.einsum("sfkb,bq->sfqk", twist_real, cos_second, precision=high) + jnp.einsum(
        "sfkb,bq->sfqk", twist_imag, sin_second, precision=high
    )
    out_imag = jnp.einsum("sfkb,bq->sfqk", twist_imag, cos_second, precision=high) - jnp.einsum(
        "sfkb,bq->sfqk", twist_real, sin_second, precision=high
    )
    norm_factor = 1.0 / jnp.sqrt(jnp.float32(span))
    out_real = out_real.reshape(stations, frames, span // 2) * norm_factor
    out_imag = out_imag.reshape(stations, frames, span // 2) * norm_factor
    phase_angle = (2.0 * jnp.pi * turn_table.astype(jnp.float32) / 65536.0)[:, :, None]
    cos_fringe = jnp.cos(phase_angle)
    sin_fringe = jnp.sin(phase_angle)
    rotated_real = out_real * cos_fringe + out_imag * sin_fringe
    rotated_imag = out_imag * cos_fringe - out_real * sin_fringe
    return jnp.stack([rotated_real, rotated_imag]).astype(jnp.bfloat16)


def cross(left_spec, right_spec):
    f32 = jnp.float32
    real_part = jnp.einsum(
        "afk,bfk->abk", left_spec[0], right_spec[0], preferred_element_type=f32
    ) + jnp.einsum("afk,bfk->abk", left_spec[1], right_spec[1], preferred_element_type=f32)
    imag_part = jnp.einsum(
        "afk,bfk->abk", left_spec[1], right_spec[0], preferred_element_type=f32
    ) - jnp.einsum("afk,bfk->abk", left_spec[0], right_spec[1], preferred_element_type=f32)
    return jnp.stack([real_part, imag_part])


def place(current_totals, block_term, first_station):
    current = lax.dynamic_slice_in_dim(current_totals, first_station, block_term.shape[2], 2)
    return lax.dynamic_update_slice_in_dim(current_totals, current + block_term, first_station, 2)


def on_device(samples, delays, fringe):
    stn_here, length = samples.shape
    frames_here = length // SPAN
    next_head = shifted(samples[:, :DMAX], "tm", -1)
    joined = jnp.concatenate([samples, next_head], axis=1)

    def take(sample_row, shift_by):
        return lax.dynamic_slice_in_dim(sample_row, shift_by, length)

    aligned = jax.vmap(take)(joined, delays[:, 0]).reshape(stn_here, frames_here, SPAN)
    own_spectra = spectrum(aligned, fringe)
    time_count = lax.axis_size("tm")
    channels_now = own_spectra.shape[3]
    cycle_size = lax.axis_size("stn")
    position = lax.axis_index("stn")
    totals = jnp.zeros((2, stn_here, stn_here * cycle_size, channels_now), jnp.float32)
    totals = place(totals, cross(own_spectra, own_spectra), position * stn_here)

    def turn_one(turn_index, state_tuple):
        current_totals, travel = state_tuple
        travel = passed_along(travel, "stn", 1)
        owner_index = (position - turn_index) % cycle_size
        current_totals = place(current_totals, cross(own_spectra, travel), owner_index * stn_here)
        return (current_totals, travel)

    totals, travel_end = lax.fori_loop(1, cycle_size, turn_one, (totals, own_spectra))
    norm_scale = 1.0 / jnp.sqrt(jnp.float32(frames_here * time_count))
    return lax.psum_scatter(totals * norm_scale, "tm", scatter_dimension=3, tiled=True)


LANES = 128
CHUNK = 4
GROUPS = ((0, 2), (3, 3))


def spectrum_tables(stn_count, tm_count):
    first = np.arange(64)
    second = np.arange(LANES)
    turn = 2.0 * np.pi * (first[:, None] * first[None, :] % 64) / 64.0
    first_table = np.concatenate([np.cos(turn), -np.sin(turn)], axis=0)
    twist = 2.0 * np.pi * (first[:, None] * second[None, :]) / SPAN
    twist_table = np.stack([np.cos(twist), -np.sin(twist)]) / np.sqrt(SPAN)
    rows = []
    for block in range(stn_count * tm_count):
        q = block * 4 + np.array([0, 2, 1, 3])
        turn = 2.0 * np.pi * (q[:, None] * second[None, :] % LANES) / LANES
        rows.append(np.concatenate([np.cos(turn), np.sin(turn)], axis=1))
        rows.append(np.concatenate([-np.sin(turn), np.cos(turn)], axis=1))
    second_table = np.concatenate(rows, axis=0)

    def halves(table):
        high = table.astype(ml_dtypes.bfloat16)
        return high, (table - high.astype(np.float64)).astype(ml_dtypes.bfloat16)

    first_table = np.concatenate(halves(first_table), axis=1)
    second_table = np.concatenate(halves(second_table), axis=0)
    return first_table, twist_table.astype(np.float32), second_table


def fused_kernel(
    S, T, norm_scale,
    samples_hbm, delays_hbm, fringe_hbm, first_hbm, twist_hbm, second_hbm,
    out_ref,
    flat, delays_ref, fringe_ref, first_ref, twist_ref, second_ref,
    signal, head, next_head, tail, outgoing, incoming, pieces, landed,
    load_sems, halo_sems, send_sem, recv_sems, last_sems,
):
    f32, bf16 = jnp.float32, jnp.bfloat16
    band = lax.axis_index("band")
    s_me = lax.axis_index("stn")
    t_me = lax.axis_index("tm")
    partners = [(ds, dt) for ds in (1, 2, 3, 0) for dt in (2, 3, 0, 1) if (ds, dt) != (0, 0)]
    late = s_me >= S // 2
    rows_chunk = CHUNK * 64
    chunks = signal.shape[0] // rows_chunk
    halo_rows = DMAX // LANES
    tail_start = (chunks - 1) * rows_chunk

    def partner(ds, dt):
        if ds == 0:
            return s_me, lax.rem(t_me + dt, T)
        upward = ds - 1 + (s_me <= ds - 1).astype(jnp.int32)
        downward = S - ds - (S - 1 - s_me <= ds - 1).astype(jnp.int32)
        return lax.select(s_me >= S // 2, upward, downward), lax.rem(t_me + dt, T)

    half = flat.shape[1] // 2
    loads = [
        pltpu.make_async_copy(source, target, load_sems.at[index])
        for index, (source, target) in enumerate(
            [
                (samples_hbm.at[:, pl.ds(0, half)], flat.at[:, pl.ds(0, half)]),
                (delays_hbm, delays_ref),
                (first_hbm, first_ref),
                (fringe_hbm, fringe_ref),
                (twist_hbm, twist_ref),
                (second_hbm, second_ref),
                (samples_hbm.at[:, pl.ds(half, half)], flat.at[:, pl.ds(half, half)]),
            ]
        )
    ]
    for load in loads:
        load.start()

    barrier = pltpu.get_barrier_semaphore()
    for ds, dt in partners:
        s_to, t_to = partner(ds, dt)
        pl.semaphore_signal(barrier, inc=1, device_id=(band, s_to, t_to), device_id_type=MESH)

    tail[pl.ds(rows_chunk + halo_rows, 8), :] = jnp.zeros((8, LANES), f32)

    @pl.when(t_me == T - 1)
    def _():
        next_head[...] = jnp.zeros_like(next_head)

    def lay_out(first_row, row_count):
        for row in range(first_row, first_row + row_count, 64):
            part = flat[:, pl.ds(row * LANES, 64 * LANES)].astype(f32).reshape(64, LANES)
            signal[pl.ds(row, 64), :] = part
            if row >= tail_start:
                tail[pl.ds(row - tail_start, 64), :] = part

    loads[0].wait()
    lay_out(0, 2 * rows_chunk)
    head[...] = signal[pl.ds(0, halo_rows), :].astype(bf16)
    loads[1].wait()
    loads[2].wait()
    loads[3].wait()
    delay = delays_ref[0, 0]
    delay_rows = delay // LANES
    delay_lanes = delay - delay_rows * LANES
    lane_from = lax.broadcasted_iota(jnp.int32, (2 * LANES, LANES), 0)
    lane_to = lax.broadcasted_iota(jnp.int32, (2 * LANES, LANES), 1)
    shift = jnp.where(lane_from == lane_to + delay_lanes, 1.0, 0.0).astype(bf16)

    phase = fringe_ref[...].astype(f32) * (2.0 * math.pi / 65536.0)
    cos_fringe = jnp.cos(phase)
    sin_fringe = jnp.sin(phase)

    def chunk_spectra(c):
        source, start = (tail, 0) if c == chunks - 1 else (signal, c * rows_chunk)
        here = source[pl.ds(delay_rows + start, rows_chunk), :].astype(bf16)
        after = source[pl.ds(delay_rows + (start + 1), rows_chunk), :].astype(bf16)
        aligned = jnp.dot(
            jnp.concatenate([here, after], axis=1), shift, preferred_element_type=f32
        ).astype(bf16)
        frames = [aligned[64 * f : 64 * (f + 1)] for f in range(CHUNK)]
        side = jnp.concatenate(frames, axis=1)
        first = jnp.dot(
            first_ref[...], jnp.concatenate([side, side], axis=0), preferred_element_type=f32
        )
        twisted = []
        for f in range(CHUNK):
            at = c * CHUNK + f
            cos_f = cos_fringe[:, at : at + 1]
            sin_f = sin_fringe[:, at : at + 1]
            twist_real = twist_ref[0] * cos_f + twist_ref[1] * sin_f
            twist_imag = twist_ref[1] * cos_f - twist_ref[0] * sin_f
            real = first[:64, LANES * f : LANES * (f + 1)]
            imag = first[64:, LANES * f : LANES * (f + 1)]
            twisted.append(
                jnp.concatenate(
                    [
                        real * twist_real - imag * twist_imag,
                        real * twist_imag + imag * twist_real,
                    ],
                    axis=1,
                )
            )
        twisted = jnp.concatenate(twisted, axis=0)
        high = twisted.astype(bf16)
        low = (twisted - high.astype(f32)).astype(bf16)
        across = (((1,), (1,)), ((), ()))
        both = lax.dot_general(second_ref[...], high, across, preferred_element_type=f32)
        small = lax.dot_general(second_ref[:LANES], low, across, preferred_element_type=f32)
        spectra = both[:LANES] + (both[LANES:] + small)
        outgoing[:, c] = jnp.concatenate(
            [
                spectra[:, :LANES].reshape(S * T, 8, LANES),
                spectra[:, LANES:].reshape(S * T, 8, LANES),
            ],
            axis=1,
        ).astype(bf16)

    def spectra_copy(group, first_chunk, last_chunk, ds, dt):
        s_to, t_to = partner(ds, dt)
        part = pl.ds(first_chunk, last_chunk + 1 - first_chunk)
        return pltpu.make_async_remote_copy(
            src_ref=outgoing.at[t_to * S + s_to, part],
            dst_ref=incoming.at[s_me * T + dt, part],
            send_sem=send_sem,
            recv_sem=recv_sems.at[group],
            device_id=(band, s_to, t_to),
            device_id_type=MESH,
        )

    def all_arrived(group):
        first_chunk, last_chunk = GROUPS[group]
        part = incoming.at[pl.ds(0, S * T - 1), pl.ds(first_chunk, last_chunk + 1 - first_chunk)]
        pltpu.make_async_copy(part, part, recv_sems.at[group]).wait()

    def halo_copy():
        return pltpu.make_async_remote_copy(
            src_ref=head,
            dst_ref=next_head,
            send_sem=halo_sems.at[0],
            recv_sem=halo_sems.at[1],
            device_id=(band, s_me, lax.rem(t_me + T - 1, T)),
            device_id_type=MESH,
        )

    for c in range(chunks):
        if c == 0:
            loads[4].wait()
            loads[5].wait()
        elif c == 1:
            loads[6].wait()
            lay_out(2 * rows_chunk, rows_chunk)
        elif c == 2:
            lay_out(3 * rows_chunk, rows_chunk)
        else:

            @pl.when(t_me < T - 1)
            def _():
                halo_copy().wait_recv()

            tail[pl.ds(rows_chunk, halo_rows), :] = next_head[...].astype(f32)

        chunk_spectra(c)
        def open_exchange():
            pl.semaphore_wait(barrier, len(partners))

            @pl.when(t_me > 0)
            def _():
                halo_copy().start()

        if c == 0:
            pl.when(late)(open_exchange)
        if c == GROUPS[0][1]:
            pl.when(jnp.logical_not(late))(open_exchange)

        if c in (0, GROUPS[0][1]):

            @pl.when(late)
            def _():
                for ds, dt in partners:
                    spectra_copy(0, min(c, 1), c, ds, dt).start()

        for group, (first_chunk, last_chunk) in enumerate(GROUPS):
            if last_chunk == c:

                @pl.when(jnp.logical_not(late) if group == 0 else True)
                def _():
                    for ds, dt in partners:
                        spectra_copy(group, first_chunk, last_chunk, ds, dt).start()

        incoming[s_me * T, c] = outgoing[t_me * S + s_me, c]

    pairs = [(i, j) for i in range(S) for j in range(i, S)]
    even = {pair: jnp.zeros((8, LANES), f32) for pair in pairs}
    odd = {pair: jnp.zeros((8, LANES), f32) for pair in pairs if pair[0] != pair[1]}
    for group, (first_chunk, last_chunk) in enumerate(GROUPS):
        all_arrived(group)
        for dt, c in [(dt, c) for dt in range(T) for c in range(first_chunk, last_chunk + 1)]:
            tiles = [incoming[s * T + dt, c].astype(f32) for s in range(S)]
            for top in (0, 8):
                part = [tile[top : top + 8] for tile in tiles]
                turned = [None] + [pltpu.roll(p, 4, 0) for p in part[1:]]
                for i, j in pairs:
                    even[i, j] += part[i] * part[j]
                    if i != j:
                        odd[i, j] += part[i] * turned[j]

    left = lax.broadcasted_iota(jnp.int32, (8, LANES), 1) < 64

    def settle(total, sign):
        total = total + pltpu.roll(total, 64, 1)
        total = (pltpu.roll(total, 4, 0) + sign * total) * norm_scale
        return jnp.where(left, total, pltpu.roll(total, 6, 0))

    def put(i, row, value):
        pieces[i, pl.ds(row, 1), pl.ds(0, LANES)] = value[0:1]
        pieces[i, pl.ds(row, 1), pl.ds(LANES, LANES)] = value[1:2]

    for i, j in pairs:
        real = settle(even[i, j], 1.0)
        put(i, j, real)
        if i == j:
            put(i, S + i, jnp.zeros_like(real))
        else:
            put(j, i, real)
            imag = settle(odd[i, j], -1.0)
            put(i, S + j, imag)
            put(j, S + i, -imag)

    def last_copy(ds):
        s_to, _ = partner(ds, 0)
        return pltpu.make_async_remote_copy(
            src_ref=pieces.at[s_to],
            dst_ref=landed.at[s_me],
            send_sem=last_sems.at[0],
            recv_sem=last_sems.at[1],
            device_id=(band, s_to, t_me),
            device_id_type=MESH,
        )

    for ds in (1, 2, 3):
        last_copy(ds).start()
    landed[s_me] = pieces[s_me]
    others = landed.at[pl.ds(0, S - 1)]
    pltpu.make_async_copy(others, others, last_sems.at[1]).wait()
    for s in range(S):
        for part in range(2):
            out_ref[part, :, pl.ds(s * 2 * LANES, 2 * LANES)] = landed[s, S * part : S * part + S]

    pltpu.make_async_copy(others, others, last_sems.at[0]).wait()
    sent = outgoing.at[pl.ds(0, S * T - 1)]
    pltpu.make_async_copy(sent, sent, send_sem).wait()

    @pl.when(t_me > 0)
    def _():
        halo_copy().wait_send()


def fused_on_device(stn_count, tm_count, samples, delays, fringe):
    length = samples.shape[1]
    rows = length // LANES
    chunks = rows // (CHUNK * 64)
    blocks = stn_count * tm_count
    norm_scale = 1.0 / math.sqrt(length // SPAN * tm_count)
    tables = spectrum_tables(stn_count, tm_count)
    operands = [samples, delays, fringe] + [jnp.asarray(table) for table in tables]
    out = pl.pallas_call(
        functools.partial(fused_kernel, stn_count, tm_count, norm_scale),
        out_shape=pltpu.VMEM((2, stn_count, 1024), jnp.float32),
        in_specs=[pl.BlockSpec(memory_space=pltpu.HBM)] * len(operands),
        out_specs=pl.BlockSpec(memory_space=pltpu.VMEM),
        scratch_shapes=[
            pltpu.VMEM(samples.shape, samples.dtype),
            pltpu.SMEM(delays.shape, delays.dtype),
        ]
        + [pltpu.VMEM(operand.shape, operand.dtype) for operand in operands[2:]]
        + [
            pltpu.VMEM((rows, LANES), jnp.float32),
            pltpu.VMEM((DMAX // LANES, LANES), jnp.bfloat16),
            pltpu.VMEM((DMAX // LANES, LANES), jnp.bfloat16),
            pltpu.VMEM((CHUNK * 64 + DMAX // LANES + 8, LANES), jnp.float32),
            pltpu.VMEM((blocks, chunks, 16, LANES), jnp.bfloat16),
            pltpu.VMEM((blocks, chunks, 16, LANES), jnp.bfloat16),
            pltpu.VMEM((stn_count, 2 * stn_count, 2 * LANES), jnp.float32),
            pltpu.VMEM((stn_count, 2 * stn_count, 2 * LANES), jnp.float32),
            pltpu.SemaphoreType.DMA((7,)),
            pltpu.SemaphoreType.DMA((2,)),
            pltpu.SemaphoreType.DMA,
            pltpu.SemaphoreType.DMA((len(GROUPS),)),
            pltpu.SemaphoreType.DMA((2,)),
        ],
        compiler_params=pltpu.CompilerParams(
            collective_id=0, has_side_effects=True, vmem_limit_bytes=60 << 20
        ),
        name="correlate",
    )(*operands)
    return out[:, None]


def solution(mesh):
    stn_count, tm_count = mesh.shape["stn"], mesh.shape["tm"]
    body = on_device
    if (stn_count, tm_count) == (4, 4):
        body = functools.partial(fused_on_device, stn_count, tm_count)
    return jax.shard_map(
        body,
        mesh=mesh,
        in_specs=(P(("band", "stn"), "tm"), P("stn", "tm"), P(("band", "stn"), "tm")),
        out_specs=P(None, ("band", "stn"), None, "tm"),
        check_vma=False,
    )
```
